32 devices in a mesh: group: 4 (over y, x), dev: 8 (over z, core).
Axes of the slice: x: 2, y: 2, z: 4, core: 2. Of those that a mesh axis runs over, the one named last changes fastest.
Arguments:
- right_side: float32 [16, 131072], P(None, ('group', 'dev')), may hold values from -6 to 6
- nugget: float32 [131072], P(('group', 'dev')), may hold values from 3 to 6
- near_blocks: bfloat16 [1024, 4, 128, 128], P(('group', 'dev')), as said below
- near_list: int32 [1024, 4], P(('group', 'dev')), may hold values from 0 to 1023, as said below
- basis: bfloat16 [1024, 64, 128], P(('group', 'dev')), may hold values from -0.5 to 0.5
- transfer: bfloat16 [1024, 4096], P(('group', 'dev')), may hold values from -0.25 to 0.25
- coupling: bfloat16 [128, 16, 4096], P(('group', 'dev')), as said below
- top_list: int32 [128, 16], P(('group', 'dev')), may hold values from 0 to 127, as said below
Outputs:
- solution_field: float32 [16, 131072], P(None, ('group', 'dev'))
- residual: float32 [16, 131072], P(None, ('group', 'dev'))
The draws below stay inside these ranges and needn't reach their ends.
Inputs may be any that keep to these rules, and one draw needn't show every extreme that they name: If near_list[i, k] = j then near_list[j, k] = i. Each entry names a leaf of the same subtree (256 leaves a subtree) at most 4 leaves away, or the leaf itself; column 0 names a leaf exactly 4 away wherever that leaf lies in the subtree. If near_list[i, k] = j then near_blocks[j, k] is near_blocks[i, k] transposed; a block of a leaf that names itself is symmetric. If top_list[c, k] = d then top_list[d, k] = c, and d differs from c. If top_list[c, k] = d then coupling[d, k] is coupling[c, k] transposed as a 64 x 64 matrix.
All inputs are finite; a program needn't handle non-finite values.
Results may differ from the reference program's by a relative error of at most 0.008.
Values may be sent and summed in bfloat16 or wider, within the bound.
No kernel may reach another device: no remote copies, remote signals or barrier semaphores. Data moves between devices by JAX's collectives and lax.ppermute only.
A program may use at most 64 MiB of HBM per device.

```python
import jax
import jax.numpy as jnp
from jax import lax

LEAF = 128
RANK = 64
RHS = 16
LEAF_DEV = 32
LEAF_CL = 8
NEAR = 4
TOPK = 16
HALO = 4
ITERS = 2
LEAVES = 1024
LEAVES_GROUP = 256
CLUSTERS = 128
SITES = 131072
DEVICES = 32


def near_partner(key):
    key_step = jax.random.fold_in(key, 11)
    key_phase = jax.random.fold_in(key, 23)
    column = jnp.arange(NEAR, dtype=jnp.int32)
    step_size = jax.random.randint(key_step, (NEAR,), 1, HALO + 1).astype(jnp.int32)
    step_size = jnp.where(column == 0, HALO, step_size).astype(jnp.int32)
    raw_phase = jax.random.randint(key_phase, (NEAR,), 0, 1048576).astype(jnp.int32)
    phase = (1 + raw_phase % (2 * step_size - 1)).astype(jnp.int32)
    leaf_ids = jnp.arange(LEAVES, dtype=jnp.int32)[:, None]
    quotient = jnp.floor_divide(leaf_ids - phase[None, :], step_size[None, :])
    target = jnp.where(quotient % 2 == 0, leaf_ids + step_size[None, :], leaf_ids - step_size[None, :])
    base = leaf_ids // LEAVES_GROUP * LEAVES_GROUP
    inside = (target >= base) & (target < base + LEAVES_GROUP)
    return jnp.where(inside, target, leaf_ids).astype(jnp.int32)


def cluster_partner(key):
    key_perm = jax.random.fold_in(key, 41)
    ids = jnp.arange(CLUSTERS, dtype=jnp.int32)

    def one_column(index):
        order = jax.random.permutation(jax.random.fold_in(key_perm, index), CLUSTERS).astype(jnp.int32)
        inverse = jnp.zeros((CLUSTERS,), jnp.int32).at[order].set(ids)
        return order[jnp.bitwise_xor(inverse, 1)].astype(jnp.int32)
    columns = jax.vmap(one_column)(jnp.arange(TOPK, dtype=jnp.int32))
    return jnp.transpose(columns).astype(jnp.int32)


def draw_near_list(key, part):
    return near_partner(key)


def draw_near_blocks(key, part):
    partner = near_partner(key)
    key_block = jax.random.fold_in(key, 31)
    leaf_ids = jnp.arange(LEAVES, dtype=jnp.int32)[:, None]
    column = jnp.arange(NEAR, dtype=jnp.int32)[None, :]
    pair_id = (jnp.minimum(leaf_ids, partner) * NEAR + column).reshape(-1)

    def one_block(index):
        return jax.random.normal(jax.random.fold_in(key_block, index), (LEAF, LEAF), jnp.float32)
    raw = jax.vmap(one_block)(pair_id).reshape(LEAVES, NEAR, LEAF, LEAF)
    flipped = jnp.swapaxes(raw, 2, 3)
    upper = (leaf_ids < partner)[:, :, None, None]
    lower = (leaf_ids > partner)[:, :, None, None]
    blocks = jnp.where(upper, raw, jnp.where(lower, flipped, (raw + flipped) * 0.70710678))
    return (blocks * (LEAF * NEAR) ** (-0.5)).astype(jnp.bfloat16)


def draw_top_list(key, part):
    return cluster_partner(key)


def draw_coupling(key, part):
    partner = cluster_partner(key)
    key_block = jax.random.fold_in(key, 77)
    cluster_ids = jnp.arange(CLUSTERS, dtype=jnp.int32)[:, None]
    column = jnp.arange(TOPK, dtype=jnp.int32)[None, :]
    pair_id = (jnp.minimum(cluster_ids, partner) * TOPK + column).reshape(-1)

    def one_block(index):
        return jax.random.normal(jax.random.fold_in(key_block, index), (RANK, RANK), jnp.float32)
    raw = jax.vmap(one_block)(pair_id).reshape(CLUSTERS, TOPK, RANK, RANK)
    flipped = jnp.swapaxes(raw, 2, 3)
    upper = (cluster_ids < partner)[:, :, None, None]
    blocks = jnp.where(upper, raw, flipped) * (RANK * TOPK) ** (-0.5)
    return blocks.reshape(CLUSTERS, TOPK, RANK * RANK).astype(jnp.bfloat16)


def steps_of(stream_key, shape, shards, least, top_value):
    loudness = 1.0
    for axis_at, shards_of in shards:
        heights = jax.random.uniform(jax.random.fold_in(jax.random.fold_in(stream_key, 6), axis_at), (shards_of,), jnp.float32, least / len(shards), top_value / len(shards))
        loudness = loudness * jnp.repeat(jnp.exp(heights), shape[axis_at] // shards_of).reshape((-1,) + (1,) * (len(shape) - 1 - axis_at))
    return loudness


def scatter_about(rng, dims, scale, bound, split=(), kind=jnp.bfloat16):
    array = jax.random.normal(rng, dims, jnp.float32) * scale
    if len(split) > 0:
        array = steps_of(rng, dims, split, -0.22, 0.18) * array
    return jnp.clip(array, min=-bound, max=bound).astype(kind)


def setup_inputs(seed: int = 0) -> dict:
    splits = jax.random.split(jax.random.key(seed), 9)
    return {
        "right_side": scatter_about(splits[0], (RHS, SITES), 1.0, 6.0, ((1, 32),), jnp.float32),
        "nugget": jnp.clip(3.0 + 3.0 * jax.random.uniform(splits[1], (SITES,), jnp.float32) ** steps_of(splits[1], (SITES,), ((0, 32),), -0.2, 0.2), 3.0, 6.0),
        "near_blocks": draw_near_blocks(jax.random.fold_in(splits[8], 71), 0),
        "near_list": draw_near_list(jax.random.fold_in(splits[8], 71), 0),
        "basis": scatter_about(splits[4], (LEAVES, RANK, LEAF), LEAF ** -0.5, 0.5, ((0, 32),)),
        "transfer": scatter_about(splits[5], (LEAVES, RANK * RANK), (RANK * LEAF_CL) ** -0.5, 0.25, ((0, 32),)),
        "coupling": draw_coupling(jax.random.fold_in(splits[8], 71), 0),
        "top_list": draw_top_list(jax.random.fold_in(splits[8], 71), 0),
    }


def operate(field, nugget, near_blocks, near_list, basis, transfer, coupling, top_list):
    vb = field.astype(jnp.bfloat16)
    leaves = vb.reshape(RHS, LEAVES, LEAF)
    blocks = near_blocks.reshape(DEVICES, LEAF_DEV, NEAR, LEAF, LEAF)
    lists = near_list.reshape(DEVICES, LEAF_DEV, NEAR)

    def one_range(args):
        block, ids = args
        values = leaves[:, ids, :]
        return jnp.einsum('lkpq,rlkq->rlp', block.astype(jnp.float32), values.astype(jnp.float32))

    near = lax.map(one_range, (blocks, lists))
    near = jnp.transpose(near, (1, 0, 2, 3)).reshape(RHS, SITES)
    coef = jnp.einsum('lap,rlp->lar', basis.astype(jnp.float32), leaves.astype(jnp.float32)).astype(jnp.bfloat16)
    emat = transfer.reshape(LEAVES, RANK, RANK).astype(jnp.float32)
    upward = jnp.einsum('lab,lar->lbr', emat, coef.astype(jnp.float32))
    upward = upward.reshape(CLUSTERS, LEAF_CL, RANK, RHS).sum(axis=1).astype(jnp.bfloat16)
    picked = upward[top_list]
    smat = coupling.reshape(CLUSTERS, TOPK, RANK, RANK).astype(jnp.float32)
    down = jnp.einsum('ckab,ckbr->car', smat, picked.astype(jnp.float32)).astype(jnp.bfloat16)
    spread = jnp.repeat(down, LEAF_CL, axis=0).astype(jnp.float32)
    local_coef = jnp.einsum('lab,lbr->lar', emat, spread).astype(jnp.bfloat16)
    far = jnp.einsum('lap,lar->rlp', basis.astype(jnp.float32), local_coef.astype(jnp.float32)).reshape(RHS, SITES)
    return nugget[None, :] * field + near + far


def reference(right_side, nugget, near_blocks, near_list, basis, transfer, coupling, top_list):
    solution_field = jnp.zeros_like(right_side)
    residual = right_side
    direction = right_side
    norm_now = jnp.sum(residual * residual, axis=1)
    for step in range(ITERS):
        image = operate(direction, nugget, near_blocks, near_list, basis, transfer, coupling, top_list)
        alpha = norm_now / jnp.sum(direction * image, axis=1)
        solution_field = solution_field + alpha[:, None] * direction
        residual = residual - alpha[:, None] * image
        norm_next = jnp.sum(residual * residual, axis=1)
        direction = residual + (norm_next / norm_now)[:, None] * direction
        norm_now = norm_next
    return solution_field, residual
```

```python
import jax
import jax.numpy as jnp
from jax import lax
from jax.sharding import PartitionSpec as P

LEAF_CL = 8
TOPK = 16
HALO = 4
AXES = ("group", "dev")


def gather_all(part):
    count = lax.axis_size("group") * lax.axis_size("dev")
    return lax.all_to_all(jnp.broadcast_to(part[None], (count,) + part.shape), AXES, 0, 0)


def halo(cells):
    ends = lax.axis_size("dev") - 1
    head = cells[:, :HALO]
    tail = cells[:, cells.shape[1] - HALO :]
    before = lax.ppermute(tail, "dev", [(i, i + 1) for i in range(ends)])
    after = lax.ppermute(head, "dev", [(i + 1, i) for i in range(ends)])
    return jnp.concatenate([before, cells, after], axis=1)


def operate(field, nugget, near_blocks, local_ids, basis, emat, smat, top_list):
    rhs_count, width = field.shape
    leaf_dev = basis.shape[0]
    leaf_size = basis.shape[2]
    rank_size = basis.shape[1]
    cl_dev = smat.shape[0]
    vb = field.astype(jnp.bfloat16).reshape(rhs_count, leaf_dev, leaf_size)
    coef = jnp.einsum("lap,rlp->lar", basis, vb, preferred_element_type=jnp.float32).astype(
        jnp.bfloat16
    )
    upward = jnp.einsum("lab,lar->lbr", emat, coef, preferred_element_type=jnp.float32)
    upward = upward.reshape(cl_dev, LEAF_CL, rank_size, rhs_count).sum(axis=1).astype(jnp.bfloat16)
    gathered = gather_all(upward.reshape(cl_dev, rank_size * rhs_count))
    gathered = gathered.reshape(-1, rank_size * rhs_count)
    values = jnp.take(halo(vb), local_ids, axis=1)
    near = jnp.einsum("lkpq,rlkq->rlp", near_blocks, values, preferred_element_type=jnp.float32)
    picked = jnp.take(gathered, top_list, axis=0).reshape(cl_dev, TOPK, rank_size, rhs_count)
    down = jnp.einsum("ckab,ckbr->car", smat, picked, preferred_element_type=jnp.float32).astype(
        jnp.bfloat16
    )
    spread = jnp.repeat(down, LEAF_CL, axis=0)
    local_coef = jnp.einsum(
        "lab,lbr->lar", emat, spread, preferred_element_type=jnp.float32
    ).astype(jnp.bfloat16)
    far = jnp.einsum("lap,lar->rlp", basis, local_coef, preferred_element_type=jnp.float32)
    return nugget[None, :] * field + (near + far).reshape(rhs_count, width)


def per_device(right_side, nugget, near_blocks, near_list, basis, transfer, coupling, top_list):
    leaf_dev = near_list.shape[0]
    rank_size = basis.shape[1]
    cl_dev = coupling.shape[0]
    first_leaf = (lax.axis_index("group") * lax.axis_size("dev") + lax.axis_index("dev")) * leaf_dev
    local_ids = near_list - first_leaf + HALO
    emat = transfer.reshape(leaf_dev, rank_size, rank_size)
    smat = coupling.reshape(cl_dev, TOPK, rank_size, rank_size)
    fixed = (nugget, near_blocks, local_ids, basis, emat, smat, top_list)
    field = right_side
    image = operate(field, *fixed)
    twice = operate(image, *fixed)

    def dot(left, right):
        return jnp.sum(left * right, axis=1)

    size = dot(image, image)
    own = dot(field, image) / jnp.where(size > 0, size, 1.0)
    rest = field - own[:, None] * image
    bent = image - own[:, None] * twice
    sums = jnp.stack(
        [
            own,
            dot(field, field),
            dot(field, image),
            dot(rest, rest),
            dot(rest, image),
            size,
            dot(rest, bent),
            dot(image, bent) + dot(rest, twice),
            dot(image, twice),
            dot(field, bent),
            dot(field, twice),
        ]
    )
    sums = gather_all(sums)
    norm = jnp.sum(sums[:, 1], axis=0)
    curve = jnp.sum(sums[:, 2], axis=0)
    alpha = norm / curve
    delta = sums[:, 0] - alpha
    norm_next = jnp.sum(sums[:, 3] + delta * (2 * sums[:, 4] + delta * sums[:, 5]), axis=0)
    beta = norm_next / norm
    rest_bent = jnp.sum(sums[:, 6] + delta * (sums[:, 7] + delta * sums[:, 8]), axis=0)
    rest_image = jnp.sum(sums[:, 4] + delta * sums[:, 5], axis=0)
    field_bent = jnp.sum(sums[:, 9] + delta * sums[:, 10], axis=0)
    curve_next = rest_bent + beta * (rest_image + field_bent + beta * curve)
    alpha_next = norm_next / curve_next
    residual = field - alpha[:, None] * image
    direction = residual + beta[:, None] * field
    solution_field = alpha[:, None] * field + alpha_next[:, None] * direction
    image_next = image - alpha[:, None] * twice + beta[:, None] * image
    return (solution_field, residual - alpha_next[:, None] * image_next)


def solution(mesh):
    placed = (
        P(None, AXES),
        P(AXES),
        P(AXES, None, None, None),
        P(AXES, None),
        P(AXES, None, None),
        P(AXES, None),
        P(AXES, None, None),
        P(AXES, None),
    )
    return jax.shard_map(
        per_device,
        mesh=mesh,
        in_specs=placed,
        out_specs=(P(None, AXES), P(None, AXES)),
        check_vma=False,
    )
```

```python
import jax
import jax.numpy as jnp
from jax import lax
from jax.experimental import pallas as pl
from jax.experimental.pallas import tpu as pltpu
from jax.sharding import PartitionSpec as P

LEAF_CL = 8
TOPK = 16
HALO = 4
AXES = ("group", "dev")
VMEM = pl.BlockSpec(memory_space=pltpu.VMEM)
SMEM = pl.BlockSpec(memory_space=pltpu.SMEM)
HBM = pl.BlockSpec(memory_space=pltpu.HBM)
PARAMS = pltpu.CompilerParams(vmem_limit_bytes=16 * 1024 * 1024)


def struct(shape, dtype):
    return jax.ShapeDtypeStruct(shape, dtype)


def in_hbm(*values):
    return [pltpu.with_memory_space_constraint(value, pltpu.HBM) for value in values]


def load_blocks(blocks_hbm, blocks_ref, sem):
    parts = sem.shape[0]
    each = blocks_ref.shape[0] // parts
    spans = [pl.ds(p * each, each) for p in range(parts)]
    copies = load_all([(blocks_hbm.at[at], blocks_ref.at[at]) for at in spans], sem)

    def ready(leaf):
        if leaf % each == 0:
            copies[leaf // each].wait()

    return ready


def load_all(pairs, sem):
    copies = [pltpu.make_async_copy(src, dst, sem.at[at]) for at, (src, dst) in enumerate(pairs)]
    for copy in copies:
        copy.start()
    return copies


def dot_tt(left, right):
    return lax.dot_general(
        left, right, (((1,), (1,)), ((), ())), preferred_element_type=jnp.float32
    )


def dot_nn(left, right):
    return lax.dot_general(
        left, right, (((1,), (0,)), ((), ())), preferred_element_type=jnp.float32
    )


def split(value):
    high = value.astype(jnp.bfloat16)
    low = (value - high.astype(jnp.float32)).astype(jnp.bfloat16)
    return jnp.concatenate([high, low], axis=0)


def put_chunk(chunk_ref, parts):
    for at in range(len(parts) // 2):
        pair = jnp.concatenate(parts[2 * at : 2 * at + 2], axis=1).astype(jnp.bfloat16)
        chunk_ref[:, at] = jnp.broadcast_to(pair[None], (chunk_ref.shape[0],) + pair.shape)


def put_halo(parity, cells, inner_ref, outer_ref):
    span = inner_ref.shape[1]
    head, tail = cells[:, :span], cells[:, cells.shape[1] - span :]

    @pl.when(parity == 0)
    def _():
        inner_ref[...] = tail
        outer_ref[...] = head

    @pl.when(parity != 0)
    def _():
        inner_ref[...] = head
        outer_ref[...] = tail


def first_kernel(
    parity_ref, field_hbm, basis_hbm, transfer_hbm,
    chunk_ref, fold_ref, cells_ref, inner_ref, outer_ref,
    field_ref, basis_ref, transfer_ref, rows_ref, emat_ref, sem,
):
    copies = load_all(
        [(transfer_hbm, transfer_ref), (basis_hbm, basis_ref), (field_hbm, field_ref)], sem
    )
    clusters, rank, span = fold_ref.shape
    leaves, _, leaf = basis_ref.shape
    rhs = field_ref.shape[0]
    lanes = 2 * rank
    copies[0].wait()
    for j in range(rank // 2):
        rows_ref[j * leaves : (j + 1) * leaves] = transfer_ref[:, j * lanes : (j + 1) * lanes].astype(jnp.float32)
    for i in range(leaves):
        rows = rows_ref[pl.ds(i, rank // 2, stride=leaves), :]
        emat_ref[i, pl.ds(0, rank // 2, stride=2), :] = rows
        emat_ref[i, pl.ds(1, rank // 2, stride=2), :] = pltpu.roll(rows, rank, 1)
    copies[1].wait()
    copies[2].wait()
    cells = split(field_ref[...])
    cells_ref[...] = cells
    put_halo(parity_ref[0], cells, inner_ref, outer_ref)
    parts = []
    for c in range(clusters):
        for i in range(LEAF_CL):
            at = c * LEAF_CL + i
            emat = emat_ref[at][:, :rank].astype(jnp.bfloat16)
            fold = lax.dot_general(
                emat, basis_ref[at], (((0,), (0,)), ((), ())), preferred_element_type=jnp.float32
            )
            fold_ref[c, :, i * leaf : (i + 1) * leaf] = fold.astype(jnp.bfloat16)
        up = dot_tt(cells[:, c * span : (c + 1) * span], fold_ref[c])
        parts.append(up[:rhs] + up[rhs:])
    put_chunk(chunk_ref, parts)


def near_sum(ids_ref, cells_ref, inner_ref, outer_ref, blocks_ref, near_ref, table, ready):
    leaves, nears, leaf, _ = blocks_ref.shape
    for i in range(leaves):
        table[i] = cells_ref[:, i * leaf : (i + 1) * leaf]
    for i in range(HALO):
        table[leaves + i] = inner_ref[:, i * leaf : (i + 1) * leaf]
        table[leaves + HALO + i] = outer_ref[:, i * leaf : (i + 1) * leaf]
    rhs = near_ref.shape[0]
    for i in range(leaves):
        ready(i)
        total = None
        for k in range(0, nears, 2):
            values = jnp.concatenate([table[ids_ref[i, k]], table[ids_ref[i, k + 1]]], axis=1)
            part = dot_tt(values, jnp.concatenate([blocks_ref[i, k], blocks_ref[i, k + 1]], axis=1))
            total = part if total is None else total + part
        near_ref[:, i * leaf : (i + 1) * leaf] = total[:rhs] + total[rhs:]


def prepare_kernel(
    ids_ref, cells_ref, inner_ref, outer_ref, fold_ref, coupling_hbm, blocks_hbm,
    near_ref, smat_ref, turned_ref, table, coupling_ref, rows_ref, blocks_ref, coupling_sem, sem,
):
    copies = load_all([(coupling_hbm, coupling_ref)], coupling_sem)
    ready = load_blocks(blocks_hbm, blocks_ref, sem)
    clusters, rank, span = fold_ref.shape
    half = rank // 2
    row = lax.broadcasted_iota(jnp.int32, (rank, rank), 0)
    column = lax.broadcasted_iota(jnp.int32, (rank, rank), 1)
    order = (column == 2 * (row % half) + row // half).astype(jnp.bfloat16)
    for c in range(clusters):
        turned_ref[c] = dot_nn(order, fold_ref[c]).astype(jnp.bfloat16)
    copies[0].wait()
    lower = lax.broadcasted_iota(jnp.int32, (half, 2 * rank), 1) < rank
    for c in range(clusters):
        for j in range(half):
            rows_ref[j * TOPK : (j + 1) * TOPK] = coupling_ref[c, :, j * 2 * rank : (j + 1) * 2 * rank].astype(jnp.float32)
        for k in range(0, TOPK, 2):
            one = rows_ref[pl.ds(k, half, stride=TOPK), :]
            two = rows_ref[pl.ds(k + 1, half, stride=TOPK), :]
            even = jnp.where(lower, one, pltpu.roll(two, rank, 1))
            odd = jnp.where(lower, pltpu.roll(one, rank, 1), two)
            smat_ref[c, :, k * rank : (k + 2) * rank] = jnp.concatenate([even, odd], axis=0).astype(jnp.bfloat16)

    near_sum(ids_ref, cells_ref, inner_ref, outer_ref, blocks_ref, near_ref, table, ready)


def near_kernel(ids_ref, cells_ref, inner_ref, outer_ref, blocks_hbm, near_ref, table, blocks_ref, sem):
    ready = load_blocks(blocks_hbm, blocks_ref, sem)
    near_sum(ids_ref, cells_ref, inner_ref, outer_ref, blocks_ref, near_ref, table, ready)


def far_part(c, top_ref, table_ref, smat_ref, turned_ref):
    rhs, lanes = table_ref.shape[2], table_ref.shape[3]
    rank = lanes // 2
    pairs = table_ref.shape[1]
    lower = lax.broadcasted_iota(jnp.int32, (rhs, lanes), 1) < rank
    pieces = []
    for k in range(0, TOPK, 2):
        halves = []
        for side in (0, 1):
            top = top_ref[c, k + side]
            pair = top // 2
            tile = table_ref[pair // pairs, pair % pairs].astype(jnp.float32)
            turned = pltpu.roll(tile, rank, 1)
            swap = jnp.broadcast_to(top % 2 != side, (rhs, lanes))
            halves.append(jnp.where(swap, turned, tile))
        pieces.append(jnp.where(lower, halves[0], halves[1]).astype(jnp.bfloat16))
    down = dot_tt(jnp.concatenate(pieces, axis=1), smat_ref[c]).astype(jnp.bfloat16)
    return dot_nn(down, turned_ref[c])


def second_kernel(
    parity_ref, top_ref, table_ref, smat_ref, turned_ref, fold_ref, nugget_ref, field_ref, near_ref,
    chunk_ref, image_ref, cells_ref, inner_ref, outer_ref,
):
    clusters, _, span = fold_ref.shape
    rhs = field_ref.shape[0]
    parts = []
    for c in range(clusters):
        at = slice(c * span, (c + 1) * span)
        far = far_part(c, top_ref, table_ref, smat_ref, turned_ref)
        image = nugget_ref[:, at] * field_ref[:, at] + near_ref[:, at] + far
        image_ref[:, at] = image
        both = split(image)
        cells_ref[:, at] = both
        up = dot_tt(both, fold_ref[c])
        parts.append(up[:rhs] + up[rhs:])
    put_chunk(chunk_ref, parts)
    put_halo(parity_ref[0], cells_ref[...], inner_ref, outer_ref)


def third_kernel(
    top_ref, table_ref, smat_ref, turned_ref, nugget_ref, field_ref, image_ref, near_ref,
    twice_ref, sums_ref,
):
    clusters, _, span = turned_ref.shape
    rhs = field_ref.shape[0]
    for c in range(clusters):
        at = slice(c * span, (c + 1) * span)
        far = far_part(c, top_ref, table_ref, smat_ref, turned_ref)
        twice_ref[:, at] = nugget_ref[:, at] * image_ref[:, at] + near_ref[:, at] + far

    def dot(left, right):
        return jnp.sum(left * right, axis=1, keepdims=True)

    field, image, twice = field_ref[...], image_ref[...], twice_ref[...]
    size = dot(image, image)
    cross = dot(field, image)
    own = cross / jnp.where(size > 0, size, 1.0)
    rest = field - own * image
    bent = image - own * twice
    sums = [
        own,
        dot(field, field),
        cross,
        dot(rest, rest),
        dot(rest, image),
        size,
        dot(rest, bent),
        dot(image, bent) + dot(rest, twice),
        dot(image, twice),
        dot(field, bent),
        dot(field, twice),
    ]
    width = sums_ref.shape[2]
    lane = lax.broadcasted_iota(jnp.int32, (rhs, width), 1)
    row = lax.broadcasted_iota(jnp.int32, (rhs, width), 0)
    packed = jnp.zeros((rhs, width), jnp.float32)
    for at, value in enumerate(sums):
        packed = jnp.where(lane == row + at * rhs, value, packed)
    flat = jnp.sum(packed, axis=0, keepdims=True)
    sums_ref[...] = jnp.broadcast_to(flat[None], sums_ref.shape)


def last_kernel(sums_ref, field_ref, image_ref, twice_ref, solution_ref, residual_ref):
    rhs = field_ref.shape[0]
    sums = sums_ref[...].reshape(sums_ref.shape[0], sums_ref.shape[2])

    def part(at):
        return sums[:, at * rhs : (at + 1) * rhs]

    def total(value):
        return jnp.sum(value, axis=0, keepdims=True)

    norm = total(part(1))
    curve = total(part(2))
    alpha = norm / curve
    delta = part(0) - alpha
    norm_next = total(part(3) + delta * (2 * part(4) + delta * part(5)))
    beta = norm_next / norm
    rest_bent = total(part(6) + delta * (part(7) + delta * part(8)))
    rest_image = total(part(4) + delta * part(5))
    field_bent = total(part(9) + delta * part(10))
    curve_next = rest_bent + beta * (rest_image + field_bent + beta * curve)
    alpha_next = norm_next / curve_next
    eye = lax.broadcasted_iota(jnp.int32, (rhs, rhs), 0) == lax.broadcasted_iota(jnp.int32, (rhs, rhs), 1)

    def column(value):
        return jnp.sum(jnp.where(eye, value, 0.0), axis=1, keepdims=True)

    alpha, beta, alpha_next = column(alpha), column(beta), column(alpha_next)
    field, image = field_ref[...], image_ref[...]
    residual = field - alpha * image
    direction = residual + beta * field
    solution_ref[...] = alpha * field + alpha_next * direction
    image_next = image - alpha * twice_ref[...] + beta * image
    residual_ref[...] = residual - alpha_next * image_next


def exchange(chunk):
    return lax.all_to_all(chunk, AXES, 0, 0)


def swap_ends(inner, outer):
    count = lax.axis_size("dev")
    inner = lax.ppermute(inner, "dev", [(i, i ^ 1) for i in range(count)])
    pairs = [(i, i + 1) for i in range(1, count - 1, 2)]
    outer = lax.ppermute(outer, "dev", pairs + [(b, a) for a, b in pairs])
    return inner, outer


def per_device(right_side, nugget, near_blocks, near_list, basis, transfer, coupling, top_list):
    rhs, width = right_side.shape
    leaves, rank, leaf = basis.shape
    clusters = coupling.shape[0]
    span = leaf * LEAF_CL
    devices = lax.axis_size("group") * lax.axis_size("dev")
    place = lax.axis_index("dev")
    parity = place % 2
    first = (lax.axis_index("group") * lax.axis_size("dev") + place) * leaves
    rel = near_list - first
    before = jnp.where(parity == 0, leaves + HALO, leaves)
    after = jnp.where(parity == 0, leaves, leaves + HALO)
    ids = jnp.where(rel < 0, rel + HALO + before, jnp.where(rel >= leaves, rel - leaves + after, rel))
    parity = parity.reshape(1).astype(jnp.int32)
    nugget = nugget[None]
    chunk_shape = struct((devices, clusters // 2, rhs, 2 * rank), jnp.bfloat16)
    end = HALO * leaf
    field_shape = pltpu.VMEM((rhs, width), jnp.float32)
    cells_shape = pltpu.VMEM((2 * rhs, width), jnp.bfloat16)
    fold_shape = pltpu.VMEM((clusters, rank, span), jnp.bfloat16)
    end_shape = struct((2 * rhs, end), jnp.bfloat16)
    table_shape = pltpu.VMEM((leaves + 2 * HALO, 2 * rhs, leaf), jnp.bfloat16)
    parts = 4

    chunk, fold, cells, inner, outer = pl.pallas_call(
        first_kernel,
        in_specs=[SMEM] + [HBM] * 3,
        out_specs=[VMEM] * 5,
        out_shape=[chunk_shape, fold_shape, cells_shape, end_shape, end_shape],
        scratch_shapes=[
            pltpu.VMEM(right_side.shape, right_side.dtype),
            pltpu.VMEM(basis.shape, basis.dtype),
            pltpu.VMEM(transfer.shape, transfer.dtype),
            pltpu.VMEM((leaves * rank // 2, 2 * rank), jnp.float32),
            pltpu.VMEM((leaves, rank, 2 * rank), jnp.float32),
            pltpu.SemaphoreType.DMA((3,)),
        ],
        compiler_params=PARAMS,
        name="first",
    )(parity, *in_hbm(right_side, basis, transfer))
    table = exchange(chunk)
    blocks = in_hbm(near_blocks)
    near, smat, turned = pl.pallas_call(
        prepare_kernel,
        in_specs=[SMEM] + [VMEM] * 4 + [HBM] * 2,
        out_specs=[VMEM] * 3,
        out_shape=[
            field_shape,
            pltpu.VMEM((clusters, rank, TOPK * rank), jnp.bfloat16),
            fold_shape,
        ],
        scratch_shapes=[
            table_shape,
            pltpu.VMEM(coupling.shape, coupling.dtype),
            pltpu.VMEM((rank // 2 * TOPK, 2 * rank), jnp.float32),
            pltpu.VMEM(near_blocks.shape, near_blocks.dtype),
            pltpu.SemaphoreType.DMA((1,)),
            pltpu.SemaphoreType.DMA((parts,)),
        ],
        compiler_params=PARAMS,
        name="prepare",
    )(ids, cells, *swap_ends(inner, outer), fold, *in_hbm(coupling), *blocks)

    chunk, image, cells, inner, outer = pl.pallas_call(
        second_kernel,
        in_specs=[SMEM] * 2 + [VMEM] * 7,
        out_specs=[VMEM] * 5,
        out_shape=[chunk_shape, field_shape, cells_shape, end_shape, end_shape],
        compiler_params=PARAMS,
        name="second",
    )(parity, top_list, table, smat, turned, fold, nugget, right_side, near)
    table = exchange(chunk)
    near = pl.pallas_call(
        near_kernel,
        in_specs=[SMEM] + [VMEM] * 3 + [HBM],
        out_specs=VMEM,
        out_shape=field_shape,
        scratch_shapes=[
            table_shape,
            pltpu.VMEM(near_blocks.shape, near_blocks.dtype),
            pltpu.SemaphoreType.DMA((parts,)),
        ],
        compiler_params=PARAMS,
        name="near",
    )(ids, cells, *swap_ends(inner, outer), *blocks)

    twice, sums = pl.pallas_call(
        third_kernel,
        in_specs=[SMEM] + [VMEM] * 7,
        out_specs=[VMEM] * 2,
        out_shape=[field_shape, struct((devices, 1, 256), jnp.float32)],
        compiler_params=PARAMS,
        name="third",
    )(top_list, table, smat, turned, nugget, right_side, image, near)
    sums = exchange(sums)

    return pl.pallas_call(
        last_kernel,
        in_specs=[VMEM] * 4,
        out_specs=[VMEM] * 2,
        out_shape=[struct((rhs, width), jnp.float32)] * 2,
        compiler_params=PARAMS,
        name="last",
    )(sums, right_side, image, twice)


def solution(mesh):
    placed = (
        P(None, AXES),
        P(AXES),
        P(AXES, None, None, None),
        P(AXES, None),
        P(AXES, None, None),
        P(AXES, None),
        P(AXES, None, None),
        P(AXES, None),
    )
    return jax.shard_map(
        per_device,
        mesh=mesh,
        in_specs=placed,
        out_specs=(P(None, AXES), P(None, AXES)),
        check_vma=False,
    )
```

```python
import functools

import jax
import jax.numpy as jnp
from jax import lax
from jax.experimental import pallas as pl
from jax.experimental.pallas import tpu as pltpu
from jax.sharding import PartitionSpec as P

LEAF_CL = 8
TOPK = 16
NEAR = 4
HALO = 4
AXES = ("group", "dev")
VMEM = pl.BlockSpec(memory_space=pltpu.VMEM)
SMEM = pl.BlockSpec(memory_space=pltpu.SMEM)
HBM = pl.BlockSpec(memory_space=pltpu.HBM)
PARAMS = pltpu.CompilerParams(vmem_limit_bytes=16 * 1024 * 1024)


def struct(shape, dtype):
    return jax.ShapeDtypeStruct(shape, dtype)


def in_hbm(*values):
    return [pltpu.with_memory_space_constraint(value, pltpu.HBM) for value in values]


def load_all(pairs, sem):
    copies = [pltpu.make_async_copy(src, dst, sem.at[at]) for at, (src, dst) in enumerate(pairs)]
    for copy in copies:
        copy.start()
    return copies


def dot_tt(left, right):
    return lax.dot_general(
        left, right, (((1,), (1,)), ((), ())), preferred_element_type=jnp.float32
    )


def dot_nn(left, right):
    return lax.dot_general(
        left, right, (((1,), (0,)), ((), ())), preferred_element_type=jnp.float32
    )


def split(value):
    high = value.astype(jnp.bfloat16)
    low = (value - high.astype(jnp.float32)).astype(jnp.bfloat16)
    return jnp.concatenate([high, low], axis=0)


def put_chunk(chunk_ref, parts):
    for at in range(len(parts) // 2):
        pair = jnp.concatenate(parts[2 * at : 2 * at + 2], axis=1).astype(jnp.bfloat16)
        chunk_ref[:, at] = jnp.broadcast_to(pair[None], (chunk_ref.shape[0],) + pair.shape)


def put_halo(parity, cells, inner_ref, outer_ref):
    span = inner_ref.shape[1]
    head, tail = cells[:, :span], cells[:, cells.shape[1] - span :]

    @pl.when(parity == 0)
    def _():
        inner_ref[...] = tail
        outer_ref[...] = head

    @pl.when(parity != 0)
    def _():
        inner_ref[...] = head
        outer_ref[...] = tail


def first_kernel(
    parity_ref, field_hbm, basis_hbm, transfer_hbm,
    chunk_ref, fold_ref, cells_ref, inner_ref, outer_ref,
    field_ref, basis_ref, transfer_ref, rows_ref, emat_ref, sem,
):
    copies = load_all(
        [(transfer_hbm, transfer_ref), (basis_hbm, basis_ref), (field_hbm, field_ref)], sem
    )
    clusters, rank, span = fold_ref.shape
    leaves, _, leaf = basis_ref.shape
    rhs = field_ref.shape[0]
    lanes = 2 * rank
    copies[0].wait()
    for j in range(rank // 2):
        rows_ref[j * leaves : (j + 1) * leaves] = transfer_ref[:, j * lanes : (j + 1) * lanes].astype(jnp.float32)
    for i in range(leaves):
        rows = rows_ref[pl.ds(i, rank // 2, stride=leaves), :]
        emat_ref[i, pl.ds(0, rank // 2, stride=2), :] = rows
        emat_ref[i, pl.ds(1, rank // 2, stride=2), :] = pltpu.roll(rows, rank, 1)
    copies[1].wait()
    copies[2].wait()
    cells = split(field_ref[...])
    cells_ref[...] = cells
    put_halo(parity_ref[0], cells, inner_ref, outer_ref)
    parts = []
    for c in range(clusters):
        for i in range(LEAF_CL):
            at = c * LEAF_CL + i
            emat = emat_ref[at][:, :rank].astype(jnp.bfloat16)
            fold = lax.dot_general(
                emat, basis_ref[at], (((0,), (0,)), ((), ())), preferred_element_type=jnp.float32
            )
            fold_ref[c, :, i * leaf : (i + 1) * leaf] = fold.astype(jnp.bfloat16)
        up = dot_tt(cells[:, c * span : (c + 1) * span], fold_ref[c])
        parts.append(up[:rhs] + up[rhs:])
    put_chunk(chunk_ref, parts)


def prepare_kernel(
    place_ref, cells_ref, fold_ref, list_hbm, coupling_hbm, blocks_hbm,
    near_ref, ends_ref, smat_ref, turned_ref, list_out, table, blocks_ref, coupling_ref, rows_ref, list_ref, sem
):
    leaves = blocks_ref.shape[0]
    starts = [0, leaves // 2]
    spans = [pl.ds(at, leaves // 2) for at in starts]
    copies = load_all(
        [(coupling_hbm, coupling_ref), (list_hbm, list_ref), (list_hbm, list_out)]
        + [(blocks_hbm.at[at], blocks_ref.at[at]) for at in spans],
        sem,
    )
    clusters, rank, span = fold_ref.shape
    half = rank // 2
    row = lax.broadcasted_iota(jnp.int32, (rank, rank), 0)
    column = lax.broadcasted_iota(jnp.int32, (rank, rank), 1)
    order = (column == 2 * (row % half) + row // half).astype(jnp.bfloat16)
    for c in range(clusters):
        turned_ref[c] = dot_nn(order, fold_ref[c]).astype(jnp.bfloat16)
    copies[0].wait()
    lower = lax.broadcasted_iota(jnp.int32, (half, 2 * rank), 1) < rank
    for c in range(clusters):
        for j in range(half):
            rows_ref[j * TOPK : (j + 1) * TOPK] = coupling_ref[c, :, j * 2 * rank : (j + 1) * 2 * rank].astype(jnp.float32)
        for k in range(0, TOPK, 2):
            one = rows_ref[pl.ds(k, half, stride=TOPK), :]
            two = rows_ref[pl.ds(k + 1, half, stride=TOPK), :]
            even = jnp.where(lower, one, pltpu.roll(two, rank, 1))
            odd = jnp.where(lower, pltpu.roll(one, rank, 1), two)
            smat_ref[c, :, k * rank : (k + 2) * rank] = jnp.concatenate([even, odd], axis=0).astype(jnp.bfloat16)
    copies[1].wait()
    copies[2].wait()

    def ready(leaf):
        if leaf in starts:
            copies[3 + starts.index(leaf)].wait()

    near_sum(place_ref, list_ref, cells_ref, blocks_ref, near_ref, ends_ref, table, ready)


def near_rows(pick, block):
    total = None
    for k in range(0, NEAR, 2):
        values = jnp.concatenate([pick(k), pick(k + 1)], axis=1)
        part = dot_tt(values, jnp.concatenate([block(k), block(k + 1)], axis=1))
        total = part if total is None else total + part
    rhs = total.shape[0] // 2
    return total[:rhs] + total[rhs:]


def near_sum(place_ref, list_ref, cells_ref, blocks_ref, near_ref, ends_ref, table, ready):
    leaves, _, leaf, _ = blocks_ref.shape
    for i in range(leaves):
        table[i] = cells_ref[:, i * leaf : (i + 1) * leaf]
    table[leaves] = jnp.zeros(table.shape[1:], table.dtype)
    first = place_ref[0]
    for i in range(leaves):
        ready(i)

        def pick(k):
            at = list_ref[k, i] - first
            return table[jnp.where((at < 0) | (at >= leaves), leaves, at)]

        near_ref[:, i * leaf : (i + 1) * leaf] = near_rows(pick, lambda k: blocks_ref[i, k])
    ends_ref[:HALO] = blocks_ref[:HALO]
    ends_ref[HALO:] = blocks_ref[leaves - HALO :]


def near_kernel(
    place_ref, list_ref, cells_ref, blocks_hbm, near_ref, ends_ref, table, blocks_ref, sem
):
    leaves = blocks_ref.shape[0]
    starts = [0, leaves // 2, leaves * 13 // 16]
    spans = [pl.ds(a, b - a) for a, b in zip(starts, starts[1:] + [leaves])]
    copies = [pltpu.make_async_copy(blocks_hbm.at[at], blocks_ref.at[at], sem.at[p]) for p, at in enumerate(spans)]
    copies[0].start()
    copies[1].start()

    def ready(leaf):
        if leaf in starts:
            at = starts.index(leaf)
            copies[at].wait()
            if at == 0:
                copies[2].start()

    near_sum(place_ref, list_ref, cells_ref, blocks_ref, near_ref, ends_ref, table, ready)


def edge_kernel(leaves, place_ref, list_ref, inner_ref, outer_ref, ends_ref, edge_ref, table):
    leaf = ends_ref.shape[2]
    zero = 2 * HALO
    table[zero] = jnp.zeros(table.shape[1:], table.dtype)
    even = jnp.where(place_ref[1] == 0, HALO, 0)
    for i in range(HALO):
        table[even + i] = inner_ref[:, i * leaf : (i + 1) * leaf]
        table[HALO - even + i] = outer_ref[:, i * leaf : (i + 1) * leaf]
    first = place_ref[0]
    for i in range(2 * HALO):
        own = i if i < HALO else leaves - 2 * HALO + i

        def pick(k):
            at = list_ref[k, own] - first
            return table[jnp.where(at < 0, at + HALO, jnp.where(at >= leaves, at - leaves + HALO, zero))]

        edge_ref[:, i * leaf : (i + 1) * leaf] = near_rows(pick, lambda k: ends_ref[i, k])


def near_part(c, clusters, near_ref, edge_ref):
    span = near_ref.shape[1] // clusters
    near = near_ref[:, c * span : (c + 1) * span]
    half = edge_ref.shape[1] // 2
    rest = jnp.zeros((near.shape[0], span - half), jnp.float32)
    if c == 0:
        near += jnp.concatenate([edge_ref[:, :half], rest], axis=1)
    if c == clusters - 1:
        near += jnp.concatenate([rest, edge_ref[:, half:]], axis=1)
    return near


def far_part(c, top_ref, table_ref, smat_ref, turned_ref):
    rhs, lanes = table_ref.shape[2], table_ref.shape[3]
    rank = lanes // 2
    pairs = table_ref.shape[1]
    lower = lax.broadcasted_iota(jnp.int32, (rhs, lanes), 1) < rank
    pieces = []
    for k in range(0, TOPK, 2):
        halves = []
        for side in (0, 1):
            top = top_ref[c, k + side]
            pair = top // 2
            tile = table_ref[pair // pairs, pair % pairs].astype(jnp.float32)
            turned = pltpu.roll(tile, rank, 1)
            swap = jnp.broadcast_to(top % 2 != side, (rhs, lanes))
            halves.append(jnp.where(swap, turned, tile))
        pieces.append(jnp.where(lower, halves[0], halves[1]).astype(jnp.bfloat16))
    down = dot_tt(jnp.concatenate(pieces, axis=1), smat_ref[c]).astype(jnp.bfloat16)
    return dot_nn(down, turned_ref[c])


def second_kernel(
    parity_ref, top_ref, table_ref, smat_ref, turned_ref, fold_ref, nugget_ref, field_ref, near_ref, edge_ref,
    chunk_ref, image_ref, cells_ref, inner_ref, outer_ref,
):
    clusters, _, span = fold_ref.shape
    rhs = field_ref.shape[0]
    parts = []
    for c in range(clusters):
        at = slice(c * span, (c + 1) * span)
        far = far_part(c, top_ref, table_ref, smat_ref, turned_ref)
        image = nugget_ref[:, at] * field_ref[:, at] + near_part(c, clusters, near_ref, edge_ref) + far
        image_ref[:, at] = image
        both = split(image)
        cells_ref[:, at] = both
        up = dot_tt(both, fold_ref[c])
        parts.append(up[:rhs] + up[rhs:])
    put_chunk(chunk_ref, parts)
    put_halo(parity_ref[0], cells_ref[...], inner_ref, outer_ref)


def third_kernel(
    top_ref, table_ref, smat_ref, turned_ref, nugget_ref, field_ref, image_ref, near_ref, edge_ref,
    twice_ref, sums_ref,
):
    clusters, _, span = turned_ref.shape
    rhs = field_ref.shape[0]
    for c in range(clusters):
        at = slice(c * span, (c + 1) * span)
        far = far_part(c, top_ref, table_ref, smat_ref, turned_ref)
        near = near_part(c, clusters, near_ref, edge_ref)
        twice_ref[:, at] = nugget_ref[:, at] * image_ref[:, at] + near + far

    def dot(left, right):
        return jnp.sum(left * right, axis=1, keepdims=True)

    field, image, twice = field_ref[...], image_ref[...], twice_ref[...]
    size = dot(image, image)
    cross = dot(field, image)
    own = cross / jnp.where(size > 0, size, 1.0)
    rest = field - own * image
    bent = image - own * twice
    sums = [
        own,
        dot(field, field),
        cross,
        dot(rest, rest),
        dot(rest, image),
        size,
        dot(rest, bent),
        dot(image, bent) + dot(rest, twice),
        dot(image, twice),
        dot(field, bent),
        dot(field, twice),
    ]
    width = sums_ref.shape[2]
    lane = lax.broadcasted_iota(jnp.int32, (rhs, width), 1)
    row = lax.broadcasted_iota(jnp.int32, (rhs, width), 0)
    packed = jnp.zeros((rhs, width), jnp.float32)
    for at, value in enumerate(sums):
        packed = jnp.where(lane == row + at * rhs, value, packed)
    flat = jnp.sum(packed, axis=0, keepdims=True)
    sums_ref[...] = jnp.broadcast_to(flat[None], sums_ref.shape)


def last_kernel(sums_ref, field_ref, image_ref, twice_ref, solution_ref, residual_ref):
    rhs = field_ref.shape[0]
    sums = sums_ref[...].reshape(sums_ref.shape[0], sums_ref.shape[2])

    def part(at):
        return sums[:, at * rhs : (at + 1) * rhs]

    def total(value):
        return jnp.sum(value, axis=0, keepdims=True)

    norm = total(part(1))
    curve = total(part(2))
    alpha = norm / curve
    delta = part(0) - alpha
    norm_next = total(part(3) + delta * (2 * part(4) + delta * part(5)))
    beta = norm_next / norm
    rest_bent = total(part(6) + delta * (part(7) + delta * part(8)))
    rest_image = total(part(4) + delta * part(5))
    field_bent = total(part(9) + delta * part(10))
    curve_next = rest_bent + beta * (rest_image + field_bent + beta * curve)
    alpha_next = norm_next / curve_next
    eye = lax.broadcasted_iota(jnp.int32, (rhs, rhs), 0) == lax.broadcasted_iota(jnp.int32, (rhs, rhs), 1)

    def column(value):
        return jnp.sum(jnp.where(eye, value, 0.0), axis=1, keepdims=True)

    alpha, beta, alpha_next = column(alpha), column(beta), column(alpha_next)
    field, image = field_ref[...], image_ref[...]
    residual = field - alpha * image
    direction = residual + beta * field
    solution_ref[...] = alpha * field + alpha_next * direction
    image_next = image - alpha * twice_ref[...] + beta * image
    residual_ref[...] = residual - alpha_next * image_next


def exchange(chunk):
    return lax.all_to_all(chunk, AXES, 0, 0)


def swap_cores(value):
    return lax.ppermute(value, "dev", [(i, i ^ 1) for i in range(lax.axis_size("dev"))])


def swap_ends(inner, outer):
    count = lax.axis_size("dev")
    inner = swap_cores(inner)
    pairs = [(i, i + 1) for i in range(1, count - 1, 2)]
    outer = lax.ppermute(outer, "dev", pairs + [(b, a) for a, b in pairs])
    return inner, outer


def per_device(right_side, nugget, near_blocks, near_list, basis, transfer, coupling, top_list):
    rhs, width = right_side.shape
    leaves, rank, leaf = basis.shape
    clusters = coupling.shape[0]
    span = leaf * LEAF_CL
    devices = lax.axis_size("group") * lax.axis_size("dev")
    place = lax.axis_index("dev")
    parity = place % 2
    first = (lax.axis_index("group") * lax.axis_size("dev") + place) * leaves
    parity = parity.reshape(1).astype(jnp.int32)
    place = jnp.stack([first, parity[0]]).astype(jnp.int32)
    near_list = near_list.T
    nugget = nugget[None]
    chunk_shape = struct((devices, clusters // 2, rhs, 2 * rank), jnp.bfloat16)
    end = HALO * leaf
    field_shape = pltpu.VMEM((rhs, width), jnp.float32)
    cells_shape = pltpu.VMEM((2 * rhs, width), jnp.bfloat16)
    fold_shape = pltpu.VMEM((clusters, rank, span), jnp.bfloat16)
    end_shape = struct((2 * rhs, end), jnp.bfloat16)

    chunk, fold, cells, inner, outer = pl.pallas_call(
        first_kernel,
        in_specs=[SMEM] + [HBM] * 3,
        out_specs=[VMEM] * 5,
        out_shape=[chunk_shape, fold_shape, cells_shape, end_shape, end_shape],
        scratch_shapes=[
            pltpu.VMEM(right_side.shape, right_side.dtype),
            pltpu.VMEM(basis.shape, basis.dtype),
            pltpu.VMEM(transfer.shape, transfer.dtype),
            pltpu.VMEM((leaves * rank // 2, 2 * rank), jnp.float32),
            pltpu.VMEM((leaves, rank, 2 * rank), jnp.float32),
            pltpu.SemaphoreType.DMA((3,)),
        ],
        compiler_params=PARAMS,
        name="first",
    )(parity, *in_hbm(right_side, basis, transfer))
    table = exchange(chunk)
    ends_shape = pltpu.VMEM((2 * HALO,) + near_blocks.shape[1:], near_blocks.dtype)
    near_scratch = [
        pltpu.VMEM((leaves + 1, 2 * rhs, leaf), jnp.bfloat16),
        pltpu.VMEM(near_blocks.shape, near_blocks.dtype),
    ]

    def edge_product(near_list, inner, outer, ends):
        return pl.pallas_call(
            functools.partial(edge_kernel, leaves),
            in_specs=[SMEM] * 2 + [VMEM] * 3,
            out_specs=VMEM,
            out_shape=pltpu.VMEM((rhs, 2 * end), jnp.float32),
            scratch_shapes=[pltpu.VMEM((2 * HALO + 1, 2 * rhs, leaf), jnp.bfloat16)],
            compiler_params=PARAMS,
            name="edge",
        )(place, near_list, *swap_ends(inner, outer), ends)

    near, ends, smat, turned, near_list = pl.pallas_call(
        prepare_kernel,
        in_specs=[SMEM] + [VMEM] * 2 + [HBM] * 3,
        out_specs=[VMEM] * 5,
        out_shape=[
            field_shape,
            ends_shape,
            pltpu.VMEM((clusters, rank, TOPK * rank), jnp.bfloat16),
            fold_shape,
            pltpu.VMEM(near_list.shape, near_list.dtype),
        ],
        scratch_shapes=near_scratch
        + [
            pltpu.VMEM(coupling.shape, coupling.dtype),
            pltpu.VMEM((rank // 2 * TOPK, 2 * rank), jnp.float32),
            pltpu.SMEM(near_list.shape, near_list.dtype),
            pltpu.SemaphoreType.DMA((5,)),
        ],
        compiler_params=PARAMS,
        name="prepare",
    )(place, cells, fold, *in_hbm(near_list, coupling, near_blocks))
    edge = edge_product(near_list, inner, outer, ends)

    chunk, image, cells, inner, outer = pl.pallas_call(
        second_kernel,
        in_specs=[SMEM] * 2 + [VMEM] * 8,
        out_specs=[VMEM] * 5,
        out_shape=[chunk_shape, field_shape, cells_shape, end_shape, end_shape],
        compiler_params=PARAMS,
        name="second",
    )(parity, top_list, table, smat, turned, fold, nugget, right_side, near, edge)
    table = exchange(chunk)
    near, ends = pl.pallas_call(
        near_kernel,
        in_specs=[SMEM] * 2 + [VMEM, HBM],
        out_specs=[VMEM] * 2,
        out_shape=[field_shape, ends_shape],
        scratch_shapes=near_scratch + [pltpu.SemaphoreType.DMA((3,))],
        compiler_params=PARAMS,
        name="near",
    )(place, near_list, cells, *in_hbm(near_blocks))
    edge = edge_product(near_list, inner, outer, ends)

    twice, sums = pl.pallas_call(
        third_kernel,
        in_specs=[SMEM] + [VMEM] * 8,
        out_specs=[VMEM] * 2,
        out_shape=[field_shape, struct((devices, 1, 256), jnp.float32)],
        compiler_params=PARAMS,
        name="third",
    )(top_list, table, smat, turned, nugget, right_side, image, near, edge)
    sums = exchange(sums)

    return pl.pallas_call(
        last_kernel,
        in_specs=[VMEM] * 4,
        out_specs=[VMEM] * 2,
        out_shape=[struct((rhs, width), jnp.float32)] * 2,
        compiler_params=PARAMS,
        name="last",
    )(sums, right_side, image, twice)


def solution(mesh):
    placed = (
        P(None, AXES),
        P(AXES),
        P(AXES, None, None, None),
        P(AXES, None),
        P(AXES, None, None),
        P(AXES, None),
        P(AXES, None, None),
        P(AXES, None),
    )
    return jax.shard_map(
        per_device,
        mesh=mesh,
        in_specs=placed,
        out_specs=(P(None, AXES), P(None, AXES)),
        check_vma=False,
    )
```

```python
import functools

import jax
import jax.numpy as jnp
from jax import lax
from jax.experimental import pallas as pl
from jax.experimental.pallas import tpu as pltpu
from jax.sharding import PartitionSpec as P

LEAF_CL = 8
TOPK = 16
NEAR = 4
HALO = 4
AXES = ("group", "dev")
VMEM = pl.BlockSpec(memory_space=pltpu.VMEM)
SMEM = pl.BlockSpec(memory_space=pltpu.SMEM)
HBM = pl.BlockSpec(memory_space=pltpu.HBM)
PARAMS = pltpu.CompilerParams(vmem_limit_bytes=16 * 1024 * 1024)


def struct(shape, dtype):
    return jax.ShapeDtypeStruct(shape, dtype)


def in_hbm(*values):
    return [pltpu.with_memory_space_constraint(value, pltpu.HBM) for value in values]


def load_all(pairs, sem):
    copies = [pltpu.make_async_copy(src, dst, sem.at[at]) for at, (src, dst) in enumerate(pairs)]
    for copy in copies:
        copy.start()
    return copies


def dot_tt(left, right):
    return lax.dot_general(
        left, right, (((1,), (1,)), ((), ())), preferred_element_type=jnp.float32
    )


def dot_nn(left, right):
    return lax.dot_general(
        left, right, (((1,), (0,)), ((), ())), preferred_element_type=jnp.float32
    )


def split(value):
    high = value.astype(jnp.bfloat16)
    low = (value - high.astype(jnp.float32)).astype(jnp.bfloat16)
    return jnp.concatenate([high, low], axis=0)


def put_chunk(chunk_ref, parts):
    for at in range(len(parts) // 2):
        pair = jnp.concatenate(parts[2 * at : 2 * at + 2], axis=1).astype(jnp.bfloat16)
        chunk_ref[:, at] = jnp.broadcast_to(pair[None], (chunk_ref.shape[0],) + pair.shape)


def put_halo(parity, cells, inner_ref, outer_ref):
    span = inner_ref.shape[1]
    head, tail = cells[:, :span], cells[:, cells.shape[1] - span :]

    @pl.when(parity == 0)
    def _():
        inner_ref[...] = tail
        outer_ref[...] = head

    @pl.when(parity != 0)
    def _():
        inner_ref[...] = head
        outer_ref[...] = tail


def first_kernel(
    parity_ref, field_hbm, basis_hbm, transfer_hbm,
    chunk_ref, fold_ref, cells_ref, inner_ref, outer_ref,
    field_ref, basis_ref, transfer_ref, rows_ref, emat_ref, sem,
):
    copies = load_all(
        [(transfer_hbm, transfer_ref), (basis_hbm, basis_ref), (field_hbm, field_ref)], sem
    )
    clusters, rank, span = fold_ref.shape
    leaves, _, leaf = basis_ref.shape
    rhs = field_ref.shape[0]
    lanes = 2 * rank
    copies[0].wait()
    for j in range(rank // 2):
        rows_ref[j * leaves : (j + 1) * leaves] = transfer_ref[:, j * lanes : (j + 1) * lanes].astype(jnp.float32)
    for i in range(leaves):
        rows = rows_ref[pl.ds(i, rank // 2, stride=leaves), :]
        emat_ref[i, pl.ds(0, rank // 2, stride=2), :] = rows
        emat_ref[i, pl.ds(1, rank // 2, stride=2), :] = pltpu.roll(rows, rank, 1)
    copies[1].wait()
    copies[2].wait()
    cells = split(field_ref[...])
    cells_ref[...] = cells
    put_halo(parity_ref[0], cells, inner_ref, outer_ref)
    folds = []
    for c in range(clusters):
        tiles = []
        for at in range(c * LEAF_CL, (c + 1) * LEAF_CL):
            emat = emat_ref[at][:, :rank].astype(jnp.bfloat16)
            fold = lax.dot_general(
                emat, basis_ref[at], (((0,), (0,)), ((), ())), preferred_element_type=jnp.float32
            )
            tiles.append(fold.astype(jnp.bfloat16))
        folds.append(jnp.concatenate(tiles, axis=1))
        fold_ref[c] = folds[c]
    parts = []
    for c, fold in enumerate(folds):
        up = dot_tt(cells[:, c * span : (c + 1) * span], fold)
        parts.append(up[:rhs] + up[rhs:])
    put_chunk(chunk_ref, parts)


def prepare_kernel(
    place_ref, cells_ref, fold_ref, top_hbm, list_hbm, coupling_hbm, blocks_hbm,
    near_ref, ends_ref, smat_ref, turned_ref, list_out,
    table, blocks_ref, coupling_ref, rows_ref, top_ref, list_ref, sem
):
    leaves = blocks_ref.shape[0]
    starts = [0, leaves // 2]
    spans = [pl.ds(at, leaves // 2) for at in starts]
    copies = load_all(
        [(top_hbm, top_ref), (coupling_hbm, coupling_ref), (list_hbm, list_ref), (list_hbm, list_out)]
        + [(blocks_hbm.at[at], blocks_ref.at[at]) for at in spans],
        sem,
    )
    clusters, rank, span = fold_ref.shape
    half = rank // 2
    row = lax.broadcasted_iota(jnp.int32, (rank, rank), 0)
    column = lax.broadcasted_iota(jnp.int32, (rank, rank), 1)
    order = (column == 2 * (row % half) + row // half).astype(jnp.bfloat16)
    for c in range(clusters):
        turned_ref[c] = dot_nn(order, fold_ref[c]).astype(jnp.bfloat16)
    copies[0].wait()
    copies[1].wait()
    lower = lax.broadcasted_iota(jnp.int32, (half, 2 * rank), 1) < rank
    for c in range(clusters):
        for j in range(half):
            rows_ref[j * TOPK : (j + 1) * TOPK] = coupling_ref[c, :, j * 2 * rank : (j + 1) * 2 * rank].astype(jnp.float32)
        for k in range(TOPK):
            rows = rows_ref[pl.ds(k, half, stride=TOPK), :]
            upper = jnp.broadcast_to(top_ref[c, k] % 2, lower.shape) == 1
            here = lower != upper
            turned = pltpu.roll(rows, rank, 1)
            even = jnp.where(here, jnp.where(upper, turned, rows), 0.0)
            odd = jnp.where(here, jnp.where(upper, rows, turned), 0.0)
            at = slice(k * 2 * rank, (k + 1) * 2 * rank)
            smat_ref[c, :, at] = jnp.concatenate([even, odd], axis=0).astype(jnp.bfloat16)
    copies[2].wait()
    copies[3].wait()

    def ready(leaf):
        if leaf in starts:
            copies[4 + starts.index(leaf)].wait()

    near_sum(place_ref, list_ref, cells_ref, blocks_ref, near_ref, ends_ref, table, ready)


def near_rows(pick, block):
    total = None
    for k in range(0, NEAR, 2):
        values = jnp.concatenate([pick(k), pick(k + 1)], axis=1)
        part = dot_tt(values, jnp.concatenate([block(k), block(k + 1)], axis=1))
        total = part if total is None else total + part
    rhs = total.shape[0] // 2
    return total[:rhs] + total[rhs:]


def near_sum(place_ref, list_ref, cells_ref, blocks_ref, near_ref, ends_ref, table, ready):
    leaves, _, leaf, _ = blocks_ref.shape
    for i in range(leaves):
        table[i] = cells_ref[:, i * leaf : (i + 1) * leaf]
    table[leaves] = jnp.zeros(table.shape[1:], table.dtype)
    first = place_ref[0]
    for i in range(leaves):
        ready(i)

        def pick(k):
            at = list_ref[k, i] - first
            return table[jnp.where((at < 0) | (at >= leaves), leaves, at)]

        near_ref[:, i * leaf : (i + 1) * leaf] = near_rows(pick, lambda k: blocks_ref[i, k])
    ends_ref[:HALO] = blocks_ref[:HALO]
    ends_ref[HALO:] = blocks_ref[leaves - HALO :]


def near_kernel(
    place_ref, list_ref, cells_ref, blocks_hbm, near_ref, ends_ref, table, blocks_ref, sem
):
    leaves = blocks_ref.shape[0]
    starts = [0, leaves // 2, leaves * 13 // 16]
    spans = [pl.ds(a, b - a) for a, b in zip(starts, starts[1:] + [leaves])]
    copies = [pltpu.make_async_copy(blocks_hbm.at[at], blocks_ref.at[at], sem.at[p]) for p, at in enumerate(spans)]
    copies[0].start()
    copies[1].start()

    def ready(leaf):
        if leaf in starts:
            at = starts.index(leaf)
            copies[at].wait()
            if at == 0:
                copies[2].start()

    near_sum(place_ref, list_ref, cells_ref, blocks_ref, near_ref, ends_ref, table, ready)


def edge_kernel(leaves, place_ref, list_ref, inner_ref, outer_ref, ends_ref, edge_ref, table):
    leaf = ends_ref.shape[2]
    zero = 2 * HALO
    table[zero] = jnp.zeros(table.shape[1:], table.dtype)
    even = jnp.where(place_ref[1] == 0, HALO, 0)
    for i in range(HALO):
        table[even + i] = inner_ref[:, i * leaf : (i + 1) * leaf]
        table[HALO - even + i] = outer_ref[:, i * leaf : (i + 1) * leaf]
    first = place_ref[0]
    for i in range(2 * HALO):
        own = i if i < HALO else leaves - 2 * HALO + i

        def pick(k):
            at = list_ref[k, own] - first
            return table[jnp.where(at < 0, at + HALO, jnp.where(at >= leaves, at - leaves + HALO, zero))]

        edge_ref[:, i * leaf : (i + 1) * leaf] = near_rows(pick, lambda k: ends_ref[i, k])


def near_part(c, clusters, near_ref, edge_ref):
    span = near_ref.shape[1] // clusters
    near = near_ref[:, c * span : (c + 1) * span]
    half = edge_ref.shape[1] // 2
    rest = jnp.zeros((near.shape[0], span - half), jnp.float32)
    if c == 0:
        near += jnp.concatenate([edge_ref[:, :half], rest], axis=1)
    if c == clusters - 1:
        near += jnp.concatenate([rest, edge_ref[:, half:]], axis=1)
    return near


def far_parts(top_ref, table_ref, smat_ref, turned_ref):
    downs = []
    for c in range(turned_ref.shape[0]):
        tiles = [table_ref[top_ref[c, k] >> 1] for k in range(TOPK)]
        downs.append(dot_tt(jnp.concatenate(tiles, axis=1), smat_ref[c]).astype(jnp.bfloat16))
    return [dot_nn(down, turned_ref[c]) for c, down in enumerate(downs)]


def second_kernel(
    parity_ref, top_ref, table_ref, smat_ref, turned_ref, fold_ref, nugget_ref, field_ref, near_ref, edge_ref,
    chunk_ref, image_ref, cells_ref, inner_ref, outer_ref,
):
    clusters, _, span = fold_ref.shape
    rhs = field_ref.shape[0]
    parts = []
    fars = far_parts(top_ref, table_ref, smat_ref, turned_ref)
    for c, far in enumerate(fars):
        at = slice(c * span, (c + 1) * span)
        image = nugget_ref[:, at] * field_ref[:, at] + near_part(c, clusters, near_ref, edge_ref) + far
        image_ref[:, at] = image
        both = split(image)
        cells_ref[:, at] = both
        up = dot_tt(both, fold_ref[c])
        parts.append(up[:rhs] + up[rhs:])
    put_chunk(chunk_ref, parts)
    put_halo(parity_ref[0], cells_ref[...], inner_ref, outer_ref)


def third_kernel(
    top_ref, table_ref, smat_ref, turned_ref, nugget_ref, field_ref, image_ref, near_ref, edge_ref,
    twice_ref, sums_ref,
):
    clusters, _, span = turned_ref.shape
    rhs = field_ref.shape[0]
    for c, far in enumerate(far_parts(top_ref, table_ref, smat_ref, turned_ref)):
        at = slice(c * span, (c + 1) * span)
        near = near_part(c, clusters, near_ref, edge_ref)
        twice_ref[:, at] = nugget_ref[:, at] * image_ref[:, at] + near + far

    def dot(left, right):
        return jnp.sum(left * right, axis=1, keepdims=True)

    field, image, twice = field_ref[...], image_ref[...], twice_ref[...]
    size = dot(image, image)
    cross = dot(field, image)
    own = cross / jnp.where(size > 0, size, 1.0)
    rest = field - own * image
    bent = image - own * twice
    sums = [
        own,
        dot(field, field),
        cross,
        dot(rest, rest),
        dot(rest, image),
        size,
        dot(rest, bent),
        dot(image, bent) + dot(rest, twice),
        dot(image, twice),
        dot(field, bent),
        dot(field, twice),
    ]
    width = sums_ref.shape[2]
    lane = lax.broadcasted_iota(jnp.int32, (rhs, width), 1)
    row = lax.broadcasted_iota(jnp.int32, (rhs, width), 0)
    packed = jnp.zeros((rhs, width), jnp.float32)
    for at, value in enumerate(sums):
        packed = jnp.where(lane == row + at * rhs, value, packed)
    flat = jnp.sum(packed, axis=0, keepdims=True)
    sums_ref[...] = jnp.broadcast_to(flat[None], sums_ref.shape)


def last_kernel(sums_ref, field_ref, image_ref, twice_ref, solution_ref, residual_ref):
    rhs = field_ref.shape[0]
    sums = sums_ref[...].reshape(sums_ref.shape[0], sums_ref.shape[2])

    def part(at):
        return sums[:, at * rhs : (at + 1) * rhs]

    def total(value):
        return jnp.sum(value, axis=0, keepdims=True)

    norm = total(part(1))
    curve = total(part(2))
    alpha = norm / curve
    delta = part(0) - alpha
    norm_next = total(part(3) + delta * (2 * part(4) + delta * part(5)))
    beta = norm_next / norm
    rest_bent = total(part(6) + delta * (part(7) + delta * part(8)))
    rest_image = total(part(4) + delta * part(5))
    field_bent = total(part(9) + delta * part(10))
    curve_next = rest_bent + beta * (rest_image + field_bent + beta * curve)
    alpha_next = norm_next / curve_next
    eye = lax.broadcasted_iota(jnp.int32, (rhs, rhs), 0) == lax.broadcasted_iota(jnp.int32, (rhs, rhs), 1)

    def column(value):
        return jnp.sum(jnp.where(eye, value, 0.0), axis=1, keepdims=True)

    alpha, beta, alpha_next = column(alpha), column(beta), column(alpha_next)
    field, image = field_ref[...], image_ref[...]
    residual = field - alpha * image
    direction = residual + beta * field
    solution_ref[...] = alpha * field + alpha_next * direction
    image_next = image - alpha * twice_ref[...] + beta * image
    residual_ref[...] = residual - alpha_next * image_next


def exchange(chunk):
    return lax.all_to_all(chunk, AXES, 0, 0)


def swap_cores(value):
    return lax.ppermute(value, "dev", [(i, i ^ 1) for i in range(lax.axis_size("dev"))])


def swap_ends(inner, outer):
    count = lax.axis_size("dev")
    inner = swap_cores(inner)
    pairs = [(i, i + 1) for i in range(1, count - 1, 2)]
    outer = lax.ppermute(outer, "dev", pairs + [(b, a) for a, b in pairs])
    return inner, outer


def per_device(right_side, nugget, near_blocks, near_list, basis, transfer, coupling, top_list):
    rhs, width = right_side.shape
    leaves, rank, leaf = basis.shape
    clusters = coupling.shape[0]
    span = leaf * LEAF_CL
    devices = lax.axis_size("group") * lax.axis_size("dev")
    place = lax.axis_index("dev")
    parity = place % 2
    first = (lax.axis_index("group") * lax.axis_size("dev") + place) * leaves
    parity = parity.reshape(1).astype(jnp.int32)
    place = jnp.stack([first, parity[0]]).astype(jnp.int32)
    near_list = near_list.T
    nugget = nugget[None]
    chunk_shape = struct((devices, clusters // 2, rhs, 2 * rank), jnp.bfloat16)
    end = HALO * leaf
    field_shape = pltpu.VMEM((rhs, width), jnp.float32)
    cells_shape = pltpu.VMEM((2 * rhs, width), jnp.bfloat16)
    fold_shape = pltpu.VMEM((clusters, rank, span), jnp.bfloat16)
    end_shape = pltpu.HBM((2 * rhs, end), jnp.bfloat16)

    chunk, fold, cells, inner, outer = pl.pallas_call(
        first_kernel,
        in_specs=[SMEM] + [HBM] * 3,
        out_specs=[VMEM] * 5,
        out_shape=[chunk_shape, fold_shape, cells_shape, end_shape, end_shape],
        scratch_shapes=[
            pltpu.VMEM(right_side.shape, right_side.dtype),
            pltpu.VMEM(basis.shape, basis.dtype),
            pltpu.VMEM(transfer.shape, transfer.dtype),
            pltpu.VMEM((leaves * rank // 2, 2 * rank), jnp.float32),
            pltpu.VMEM((leaves, rank, 2 * rank), jnp.float32),
            pltpu.SemaphoreType.DMA((3,)),
        ],
        compiler_params=PARAMS,
        name="first",
    )(parity, *in_hbm(right_side, basis, transfer))
    table = exchange(chunk).reshape(-1, rhs, 2 * rank)
    ends_shape = pltpu.VMEM((2 * HALO,) + near_blocks.shape[1:], near_blocks.dtype)
    near_scratch = [
        pltpu.VMEM((leaves + 1, 2 * rhs, leaf), jnp.bfloat16),
        pltpu.VMEM(near_blocks.shape, near_blocks.dtype),
    ]

    def edge_product(near_list, inner, outer, ends):
        return pl.pallas_call(
            functools.partial(edge_kernel, leaves),
            in_specs=[SMEM] * 2 + [VMEM] * 3,
            out_specs=VMEM,
            out_shape=pltpu.VMEM((rhs, 2 * end), jnp.float32),
            scratch_shapes=[pltpu.VMEM((2 * HALO + 1, 2 * rhs, leaf), jnp.bfloat16)],
            compiler_params=PARAMS,
            name="edge",
        )(place, near_list, *swap_ends(inner, outer), ends)

    near, ends, smat, turned, near_list = pl.pallas_call(
        prepare_kernel,
        in_specs=[SMEM] + [VMEM] * 2 + [HBM] * 4,
        out_specs=[VMEM] * 5,
        out_shape=[
            field_shape,
            ends_shape,
            pltpu.VMEM((clusters, rank, TOPK * 2 * rank), jnp.bfloat16),
            fold_shape,
            pltpu.VMEM(near_list.shape, near_list.dtype),
        ],
        scratch_shapes=near_scratch
        + [
            pltpu.VMEM(coupling.shape, coupling.dtype),
            pltpu.VMEM((rank // 2 * TOPK, 2 * rank), jnp.float32),
            pltpu.SMEM(top_list.shape, top_list.dtype),
            pltpu.SMEM(near_list.shape, near_list.dtype),
            pltpu.SemaphoreType.DMA((6,)),
        ],
        compiler_params=PARAMS,
        name="prepare",
    )(place, cells, fold, *in_hbm(top_list, near_list, coupling, near_blocks))
    edge = edge_product(near_list, inner, outer, ends)

    chunk, image, cells, inner, outer = pl.pallas_call(
        second_kernel,
        in_specs=[SMEM] * 2 + [VMEM] * 8,
        out_specs=[VMEM] * 5,
        out_shape=[chunk_shape, field_shape, cells_shape, end_shape, end_shape],
        compiler_params=PARAMS,
        name="second",
    )(parity, top_list, table, smat, turned, fold, nugget, right_side, near, edge)
    table = exchange(chunk).reshape(-1, rhs, 2 * rank)
    near, ends = pl.pallas_call(
        near_kernel,
        in_specs=[SMEM] * 2 + [VMEM, HBM],
        out_specs=[VMEM] * 2,
        out_shape=[field_shape, ends_shape],
        scratch_shapes=near_scratch + [pltpu.SemaphoreType.DMA((3,))],
        compiler_params=PARAMS,
        name="near",
    )(place, near_list, cells, *in_hbm(near_blocks))
    edge = edge_product(near_list, inner, outer, ends)

    twice, sums = pl.pallas_call(
        third_kernel,
        in_specs=[SMEM] + [VMEM] * 8,
        out_specs=[VMEM] * 2,
        out_shape=[field_shape, struct((devices, 1, 256), jnp.float32)],
        compiler_params=PARAMS,
        name="third",
    )(top_list, table, smat, turned, nugget, right_side, image, near, edge)
    sums = exchange(sums)

    return pl.pallas_call(
        last_kernel,
        in_specs=[VMEM] * 4,
        out_specs=[VMEM] * 2,
        out_shape=[struct((rhs, width), jnp.float32)] * 2,
        compiler_params=PARAMS,
        name="last",
    )(sums, right_side, image, twice)


def solution(mesh):
    placed = (
        P(None, AXES),
        P(AXES),
        P(AXES, None, None, None),
        P(AXES, None),
        P(AXES, None, None),
        P(AXES, None),
        P(AXES, None, None),
        P(AXES, None),
    )
    return jax.shard_map(
        per_device,
        mesh=mesh,
        in_specs=placed,
        out_specs=(P(None, AXES), P(None, AXES)),
        check_vma=False,
    )
```

```python
import functools

import jax
import jax.numpy as jnp
from jax import lax
from jax.experimental import pallas as pl
from jax.experimental.pallas import tpu as pltpu
from jax.sharding import PartitionSpec as P

LEAF_CL = 8
TOPK = 16
NEAR = 4
PARTS = 4
HALO = 4
AXES = ("group", "dev")
VMEM = pl.BlockSpec(memory_space=pltpu.VMEM)
SMEM = pl.BlockSpec(memory_space=pltpu.SMEM)
HBM = pl.BlockSpec(memory_space=pltpu.HBM)
PARAMS = pltpu.CompilerParams(vmem_limit_bytes=16 * 1024 * 1024)


def struct(shape, dtype):
    return jax.ShapeDtypeStruct(shape, dtype)


def in_hbm(*values):
    return [pltpu.with_memory_space_constraint(value, pltpu.HBM) for value in values]


def load_all(pairs, sem):
    copies = [pltpu.make_async_copy(src, dst, sem.at[at]) for at, (src, dst) in enumerate(pairs)]
    for copy in copies:
        copy.start()
    return copies


def dot_tt(left, right):
    return lax.dot_general(
        left, right, (((1,), (1,)), ((), ())), preferred_element_type=jnp.float32
    )


def dot_nn(left, right):
    return lax.dot_general(
        left, right, (((1,), (0,)), ((), ())), preferred_element_type=jnp.float32
    )


def split(value):
    high = value.astype(jnp.bfloat16)
    low = (value - high.astype(jnp.float32)).astype(jnp.bfloat16)
    return jnp.concatenate([high, low], axis=0)


def put_chunk(chunk_ref, parts):
    for at in range(len(parts) // 2):
        pair = jnp.concatenate(parts[2 * at : 2 * at + 2], axis=1).astype(jnp.bfloat16)
        chunk_ref[:, at] = jnp.broadcast_to(pair[None], (chunk_ref.shape[0],) + pair.shape)


def put_halo(parity, cells_ref, inner_ref, outer_ref):
    span = inner_ref.shape[1]
    head, tail = cells_ref[:, :span], cells_ref[:, cells_ref.shape[1] - span :]

    @pl.when(parity == 0)
    def _():
        inner_ref[...] = tail
        outer_ref[...] = head

    @pl.when(parity != 0)
    def _():
        inner_ref[...] = head
        outer_ref[...] = tail


def first_kernel(
    field_hbm, basis_hbm, transfer_hbm, list_hbm, top_hbm,
    chunk_ref, fold_ref, cells_ref, inner_ref, outer_ref, place_ref, list_ref, top_ref,
    field_ref, basis_ref, transfer_ref, rows_ref, emat_ref, sem,
):
    clusters, rank, span = fold_ref.shape
    leaves, _, leaf = basis_ref.shape
    rhs = field_ref.shape[0]
    lanes = 2 * rank
    copies = load_all(
        [
            (transfer_hbm, transfer_ref),
            (field_hbm, field_ref),
            (basis_hbm, basis_ref),
            (list_hbm, list_ref),
            (top_hbm, top_ref),
        ],
        sem,
    )
    device = lax.axis_index("dev")
    place_ref[0] = (lax.axis_index("group") * lax.axis_size("dev") + device) * leaves
    place_ref[1] = device % 2
    copies[0].wait()
    for j in range(rank // 2):
        rows_ref[j * leaves : (j + 1) * leaves] = transfer_ref[:, j * lanes : (j + 1) * lanes].astype(jnp.float32)
    for i in range(leaves):
        rows = rows_ref[pl.ds(i, rank // 2, stride=leaves), :]
        emat_ref[i, pl.ds(0, rank // 2, stride=2), :] = rows
        emat_ref[i, pl.ds(1, rank // 2, stride=2), :] = pltpu.roll(rows, rank, 1)
    copies[1].wait()
    copies[2].wait()
    cells = split(field_ref[...])
    cells_ref[...] = cells
    folds = []
    for c in range(clusters):
        tiles = []
        for i in range(c * LEAF_CL, (c + 1) * LEAF_CL):
            emat = emat_ref[i][:, :rank].astype(jnp.bfloat16)
            fold = lax.dot_general(
                emat, basis_ref[i], (((0,), (0,)), ((), ())), preferred_element_type=jnp.float32
            )
            tiles.append(fold.astype(jnp.bfloat16))
        folds.append(jnp.concatenate(tiles, axis=1))
        fold_ref[c] = folds[c]
    parts = [halves_sum(dot_tt(cells[:, c * span : (c + 1) * span], fold)) for c, fold in enumerate(folds)]
    put_chunk(chunk_ref, parts)
    put_halo(device % 2, cells_ref, inner_ref, outer_ref)
    copies[3].wait()
    copies[4].wait()


def prepare_kernel(
    place_ref, list_ref, top_ref, cells_ref, fold_ref, coupling_hbm, blocks_hbm,
    near_ref, ends_ref, smat_ref, turned_ref, table, blocks_ref, coupling_ref, rows_ref, sem
):
    pairs, each = part_copies(blocks_hbm, blocks_ref)
    copies = load_all([(coupling_hbm, coupling_ref)] + pairs, sem)
    clusters, rank, span = fold_ref.shape
    half = rank // 2
    row = lax.broadcasted_iota(jnp.int32, (rank, rank), 0)
    column = lax.broadcasted_iota(jnp.int32, (rank, rank), 1)
    order = (column == 2 * (row % half) + row // half).astype(jnp.bfloat16)
    for c in range(clusters):
        turned_ref[c] = dot_nn(order, fold_ref[c]).astype(jnp.bfloat16)
    copies[0].wait()
    lower = lax.broadcasted_iota(jnp.int32, (half, 2 * rank), 1) < rank
    for c in range(clusters):
        for j in range(half):
            rows_ref[j * TOPK : (j + 1) * TOPK] = coupling_ref[c, :, j * 2 * rank : (j + 1) * 2 * rank].astype(jnp.float32)
        for k in range(TOPK):
            rows = rows_ref[pl.ds(k, half, stride=TOPK), :]
            upper = jnp.broadcast_to(top_ref[c, k] % 2, lower.shape) == 1
            here = lower != upper
            turned = pltpu.roll(rows, rank, 1)
            even = jnp.where(here, jnp.where(upper, turned, rows), 0.0)
            odd = jnp.where(here, jnp.where(upper, rows, turned), 0.0)
            at = slice(k * 2 * rank, (k + 1) * 2 * rank)
            smat_ref[c, :, at] = jnp.concatenate([even, odd], axis=0).astype(jnp.bfloat16)
    ready = wait_parts(copies[1:], each)
    near_sum(place_ref, list_ref, cells_ref, blocks_ref, near_ref, ends_ref, table, ready)


def halves_sum(total):
    rhs = total.shape[0] // 2
    return total[:rhs] + total[rhs:]


def near_sum(place_ref, list_ref, cells_ref, blocks_ref, near_ref, ends_ref, table, ready):
    leaves, _, leaf, _ = blocks_ref.shape
    for i in range(leaves):
        table[i] = cells_ref[:, i * leaf : (i + 1) * leaf]
    table[leaves] = jnp.zeros(table.shape[1:], table.dtype)
    first = place_ref[0]
    for i in range(leaves):
        ready(min(i + HALO, leaves - 1))
        values, blocks = [], []
        for k in range(NEAR):
            at = list_ref[k, i] - first
            inside = (at >= 0) & (at < leaves)
            values.append(table[jnp.where(inside, at, leaves)])
            blocks.append(blocks_ref[jnp.where(inside, at, i), k])
        total = dot_nn(jnp.concatenate(values, axis=1), jnp.concatenate(blocks, axis=0))
        near_ref[:, i * leaf : (i + 1) * leaf] = halves_sum(total)
    ends_ref[:HALO] = blocks_ref[:HALO]
    ends_ref[HALO:] = blocks_ref[leaves - HALO :]


def wait_parts(copies, each):
    done = []

    def ready(leaf):
        while len(done) <= leaf // each:
            copies[len(done)].wait()
            done.append(leaf)

    return ready


def part_copies(blocks_hbm, blocks_ref):
    each = blocks_ref.shape[0] // PARTS
    spans = [pl.ds(at * each, each) for at in range(PARTS)]
    return [(blocks_hbm.at[at], blocks_ref.at[at]) for at in spans], each


def near_kernel(
    place_ref, list_ref, cells_ref, blocks_hbm, near_ref, ends_ref, table, blocks_ref, sem
):
    pairs, each = part_copies(blocks_hbm, blocks_ref)
    ready = wait_parts(load_all(pairs, sem), each)
    near_sum(place_ref, list_ref, cells_ref, blocks_ref, near_ref, ends_ref, table, ready)


def edge_kernel(leaves, place_ref, list_ref, inner_ref, outer_ref, ends_ref, edge_ref, table):
    leaf = ends_ref.shape[2]
    zero = 2 * HALO
    table[zero] = jnp.zeros(table.shape[1:], table.dtype)
    even = jnp.where(place_ref[1] == 0, HALO, 0)
    for i in range(HALO):
        table[even + i] = inner_ref[:, i * leaf : (i + 1) * leaf]
        table[HALO - even + i] = outer_ref[:, i * leaf : (i + 1) * leaf]
    first = place_ref[0]
    for i in range(2 * HALO):
        own = i if i < HALO else leaves - 2 * HALO + i

        def pick(k):
            at = list_ref[k, own] - first
            return table[jnp.where(at < 0, at + HALO, jnp.where(at >= leaves, at - leaves + HALO, zero))]

        values = jnp.concatenate([pick(k) for k in range(NEAR)], axis=1)
        blocks = jnp.concatenate([ends_ref[i, k] for k in range(NEAR)], axis=1)
        edge_ref[:, i * leaf : (i + 1) * leaf] = halves_sum(dot_tt(values, blocks))


def near_part(c, clusters, near_ref, edge_ref):
    span = near_ref.shape[1] // clusters
    near = near_ref[:, c * span : (c + 1) * span]
    half = edge_ref.shape[1] // 2
    rest = jnp.zeros((near.shape[0], span - half), jnp.float32)
    if c == 0:
        near += jnp.concatenate([edge_ref[:, :half], rest], axis=1)
    if c == clusters - 1:
        near += jnp.concatenate([rest, edge_ref[:, half:]], axis=1)
    return near


def far_parts(top_ref, table_ref, smat_ref, turned_ref):
    downs = []
    for c in range(turned_ref.shape[0]):
        tiles = [table_ref[top_ref[c, k] >> 1] for k in range(TOPK)]
        downs.append(dot_tt(jnp.concatenate(tiles, axis=1), smat_ref[c]).astype(jnp.bfloat16))
    return [dot_nn(down, turned_ref[c]) for c, down in enumerate(downs)]


def second_kernel(
    place_ref, top_ref, table_ref, smat_ref, turned_ref, fold_ref, nugget_ref, field_ref, near_ref, edge_ref,
    chunk_ref, image_ref, cells_ref, inner_ref, outer_ref,
):
    clusters, _, span = fold_ref.shape
    rhs = field_ref.shape[0]
    parts = []
    fars = far_parts(top_ref, table_ref, smat_ref, turned_ref)
    for c, far in enumerate(fars):
        at = slice(c * span, (c + 1) * span)
        image = nugget_ref[:, at] * field_ref[:, at] + near_part(c, clusters, near_ref, edge_ref) + far
        image_ref[:, at] = image
        both = split(image)
        cells_ref[:, at] = both
        parts.append(halves_sum(dot_tt(both, fold_ref[c])))
    put_chunk(chunk_ref, parts)
    put_halo(place_ref[1], cells_ref, inner_ref, outer_ref)


def third_kernel(
    top_ref, table_ref, smat_ref, turned_ref, nugget_ref, field_ref, image_ref, near_ref, edge_ref,
    twice_ref, sums_ref,
):
    clusters, _, span = turned_ref.shape
    rhs = field_ref.shape[0]
    for c, far in enumerate(far_parts(top_ref, table_ref, smat_ref, turned_ref)):
        at = slice(c * span, (c + 1) * span)
        near = near_part(c, clusters, near_ref, edge_ref)
        twice_ref[:, at] = nugget_ref[:, at] * image_ref[:, at] + near + far

    def dot(left, right):
        return jnp.sum(left * right, axis=1, keepdims=True)

    field, image, twice = field_ref[...], image_ref[...], twice_ref[...]
    size = dot(image, image)
    cross = dot(field, image)
    own = cross / jnp.where(size > 0, size, 1.0)
    rest = field - own * image
    bent = image - own * twice
    sums = [
        dot(field, field),
        cross,
        size,
        dot(rest, rest),
        dot(rest, bent),
        dot(image, bent) + dot(rest, twice),
        dot(image, twice),
    ]
    width = sums_ref.shape[2]
    lane = lax.broadcasted_iota(jnp.int32, (rhs, width), 1)
    row = lax.broadcasted_iota(jnp.int32, (rhs, width), 0)
    packed = jnp.zeros((rhs, width), jnp.float32)
    for at, value in enumerate(sums):
        packed = jnp.where(lane == row + at * rhs, value, packed)
    flat = jnp.sum(packed, axis=0, keepdims=True)
    sums_ref[...] = jnp.broadcast_to(flat[None], sums_ref.shape)


def last_kernel(sums_ref, field_ref, image_ref, twice_ref, solution_ref, residual_ref):
    rhs = field_ref.shape[0]
    sums = sums_ref[...].reshape(sums_ref.shape[0], sums_ref.shape[2])

    def part(at):
        return sums[:, at * rhs : (at + 1) * rhs]

    def total(value):
        return jnp.sum(value, axis=0, keepdims=True)

    norm = total(part(0))
    curve = total(part(1))
    alpha = norm / curve
    size = part(2)
    delta = part(1) / jnp.where(size > 0, size, 1.0) - alpha
    norm_next = total(part(3) + delta * delta * size)
    beta = norm_next / norm
    rest_bent = total(part(4) + delta * (part(5) + delta * part(6)))
    rest_image = total(delta * size)
    curve_next = rest_bent + beta * (2.0 * rest_image + beta * curve)
    alpha_next = norm_next / curve_next
    eye = lax.broadcasted_iota(jnp.int32, (rhs, rhs), 0) == lax.broadcasted_iota(jnp.int32, (rhs, rhs), 1)

    def column(value):
        return jnp.sum(jnp.where(eye, value, 0.0), axis=1, keepdims=True)

    alpha, beta, alpha_next = column(alpha), column(beta), column(alpha_next)
    field, image = field_ref[...], image_ref[...]
    residual = field - alpha * image
    direction = residual + beta * field
    solution_ref[...] = alpha * field + alpha_next * direction
    image_next = image - alpha * twice_ref[...] + beta * image
    residual_ref[...] = residual - alpha_next * image_next


def exchange(chunk):
    return lax.all_to_all(chunk, AXES, 0, 0)


def swap_cores(value):
    return lax.ppermute(value, "dev", [(i, i ^ 1) for i in range(lax.axis_size("dev"))])


def swap_ends(inner, outer):
    count = lax.axis_size("dev")
    inner = swap_cores(inner)
    pairs = [(i, i + 1) for i in range(1, count - 1, 2)]
    outer = lax.ppermute(outer, "dev", pairs + [(b, a) for a, b in pairs])
    return inner, outer


def per_device(right_side, nugget, near_blocks, near_list, basis, transfer, coupling, top_list):
    rhs, width = right_side.shape
    leaves, rank, leaf = basis.shape
    clusters = coupling.shape[0]
    span = leaf * LEAF_CL
    devices = lax.axis_size("group") * lax.axis_size("dev")
    nugget = nugget[None]
    chunk_shape = struct((devices, clusters // 2, rhs, 2 * rank), jnp.bfloat16)
    end = HALO * leaf
    field_shape = pltpu.VMEM((rhs, width), jnp.float32)
    cells_shape = pltpu.VMEM((2 * rhs, width), jnp.bfloat16)
    fold_shape = pltpu.VMEM((clusters, rank, span), jnp.bfloat16)
    end_shape = pltpu.HBM((2 * rhs, end), jnp.bfloat16)

    chunk, fold, cells, inner, outer, place, near_list, top_list = pl.pallas_call(
        first_kernel,
        in_specs=[HBM] * 5,
        out_specs=[VMEM] * 5 + [SMEM] * 3,
        out_shape=[
            chunk_shape,
            fold_shape,
            cells_shape,
            end_shape,
            end_shape,
            pltpu.SMEM((2,), jnp.int32),
            pltpu.SMEM(near_list.T.shape, near_list.dtype),
            pltpu.SMEM(top_list.shape, top_list.dtype),
        ],
        scratch_shapes=[
            pltpu.VMEM(right_side.shape, right_side.dtype),
            pltpu.VMEM(basis.shape, basis.dtype),
            pltpu.VMEM(transfer.shape, transfer.dtype),
            pltpu.VMEM((leaves * rank // 2, 2 * rank), jnp.float32),
            pltpu.VMEM((leaves, rank, 2 * rank), jnp.float32),
            pltpu.SemaphoreType.DMA((5,)),
        ],
        compiler_params=PARAMS,
        name="first",
    )(*in_hbm(right_side, basis, transfer, near_list.T, top_list))
    table = exchange(chunk).reshape(-1, rhs, 2 * rank)
    ends_shape = pltpu.VMEM((2 * HALO,) + near_blocks.shape[1:], near_blocks.dtype)
    near_scratch = [
        pltpu.VMEM((leaves + 1, 2 * rhs, leaf), jnp.bfloat16),
        pltpu.VMEM(near_blocks.shape, near_blocks.dtype),
    ]

    def edge_product(inner, outer, ends):
        return pl.pallas_call(
            functools.partial(edge_kernel, leaves),
            in_specs=[SMEM] * 2 + [VMEM] * 3,
            out_specs=VMEM,
            out_shape=pltpu.VMEM((rhs, 2 * end), jnp.float32),
            scratch_shapes=[pltpu.VMEM((2 * HALO + 1, 2 * rhs, leaf), jnp.bfloat16)],
            compiler_params=PARAMS,
            name="edge",
        )(place, near_list, *swap_ends(inner, outer), ends)

    near, ends, smat, turned = pl.pallas_call(
        prepare_kernel,
        in_specs=[SMEM] * 3 + [VMEM] * 2 + [HBM] * 2,
        out_specs=[VMEM] * 4,
        out_shape=[
            field_shape,
            ends_shape,
            pltpu.VMEM((clusters, rank, TOPK * 2 * rank), jnp.bfloat16),
            fold_shape,
        ],
        scratch_shapes=near_scratch
        + [
            pltpu.VMEM(coupling.shape, coupling.dtype),
            pltpu.VMEM((rank // 2 * TOPK, 2 * rank), jnp.float32),
            pltpu.SemaphoreType.DMA((1 + PARTS,)),
        ],
        compiler_params=PARAMS,
        name="prepare",
    )(place, near_list, top_list, cells, fold, *in_hbm(coupling, near_blocks))
    edge = edge_product(inner, outer, ends)

    chunk, image, cells, inner, outer = pl.pallas_call(
        second_kernel,
        in_specs=[SMEM] * 2 + [VMEM] * 8,
        out_specs=[VMEM] * 5,
        out_shape=[chunk_shape, field_shape, cells_shape, end_shape, end_shape],
        compiler_params=PARAMS,
        name="second",
    )(place, top_list, table, smat, turned, fold, nugget, right_side, near, edge)
    table = exchange(chunk).reshape(-1, rhs, 2 * rank)
    near, ends = pl.pallas_call(
        near_kernel,
        in_specs=[SMEM] * 2 + [VMEM, HBM],
        out_specs=[VMEM] * 2,
        out_shape=[field_shape, ends_shape],
        scratch_shapes=near_scratch + [pltpu.SemaphoreType.DMA((PARTS,))],
        compiler_params=PARAMS,
        name="near",
    )(place, near_list, cells, *in_hbm(near_blocks))
    edge = edge_product(inner, outer, ends)

    twice, sums = pl.pallas_call(
        third_kernel,
        in_specs=[SMEM] + [VMEM] * 8,
        out_specs=[VMEM] * 2,
        out_shape=[field_shape, struct((devices, 1, 8 * rhs), jnp.float32)],
        compiler_params=PARAMS,
        name="third",
    )(top_list, table, smat, turned, nugget, right_side, image, near, edge)
    sums = exchange(sums)

    return pl.pallas_call(
        last_kernel,
        in_specs=[VMEM] * 4,
        out_specs=[VMEM] * 2,
        out_shape=[struct((rhs, width), jnp.float32)] * 2,
        compiler_params=PARAMS,
        name="last",
    )(sums, right_side, image, twice)


def solution(mesh):
    placed = (
        P(None, AXES),
        P(AXES),
        P(AXES, None, None, None),
        P(AXES, None),
        P(AXES, None, None),
        P(AXES, None),
        P(AXES, None, None),
        P(AXES, None),
    )
    return jax.shard_map(
        per_device,
        mesh=mesh,
        in_specs=placed,
        out_specs=(P(None, AXES), P(None, AXES)),
        check_vma=False,
    )
```

```python
import functools

import jax
import jax.numpy as jnp
from jax import lax
from jax.experimental import pallas as pl
from jax.experimental.pallas import tpu as pltpu
from jax.sharding import PartitionSpec as P

LEAF_CL = 8
TOPK = 16
NEAR = 4
PARTS = 4
HALO = 4
AXES = ("group", "dev")
VMEM = pl.BlockSpec(memory_space=pltpu.VMEM)
SMEM = pl.BlockSpec(memory_space=pltpu.SMEM)
HBM = pl.BlockSpec(memory_space=pltpu.HBM)
PARAMS = pltpu.CompilerParams(vmem_limit_bytes=16 * 1024 * 1024)


def struct(shape, dtype):
    return jax.ShapeDtypeStruct(shape, dtype)


def in_hbm(*values):
    return [pltpu.with_memory_space_constraint(value, pltpu.HBM) for value in values]


def load_all(pairs, sem):
    copies = [pltpu.make_async_copy(src, dst, sem.at[at]) for at, (src, dst) in enumerate(pairs)]
    for copy in copies:
        copy.start()
    return copies


def dot_tt(left, right):
    return lax.dot_general(
        left, right, (((1,), (1,)), ((), ())), preferred_element_type=jnp.float32
    )


def dot_nn(left, right):
    return lax.dot_general(
        left, right, (((1,), (0,)), ((), ())), preferred_element_type=jnp.float32
    )


def split(value):
    high = value.astype(jnp.bfloat16)
    low = (value - high.astype(jnp.float32)).astype(jnp.bfloat16)
    return jnp.concatenate([high, low], axis=0)


def send_chunk(chunk_hbm, chunk_ref, sem, parts):
    for at in range(len(parts) // 2):
        pair = jnp.concatenate(parts[2 * at : 2 * at + 2], axis=1).astype(jnp.bfloat16)
        chunk_ref[:, at] = jnp.broadcast_to(pair[None], (chunk_ref.shape[0],) + pair.shape)
    copy = pltpu.make_async_copy(chunk_ref, chunk_hbm, sem.at[0])
    copy.start()
    return copy


def put_halo(core, field_ref, inner_ref, outer_ref):
    span = inner_ref.shape[1]
    head, tail = split(field_ref[:, :span]), split(field_ref[:, field_ref.shape[1] - span :])

    @pl.when(core == 0)
    def _():
        inner_ref[...] = tail
        outer_ref[...] = head

    @pl.when(core != 0)
    def _():
        inner_ref[...] = head
        outer_ref[...] = tail


def first_kernel(
    field_hbm, basis_hbm, transfer_hbm, list_hbm, top_hbm,
    chunk_hbm, field_ref, fold_ref, inner_ref, outer_ref, place_ref, list_ref, top_ref,
    chunk_ref, chunk_sem, basis_ref, transfer_ref, rows_ref, emat_ref, sem,
):
    clusters, rank, span = fold_ref.shape
    leaves, _, leaf = basis_ref.shape
    rhs = field_ref.shape[0]
    lanes = 2 * rank
    copies = load_all(
        [
            (transfer_hbm, transfer_ref),
            (field_hbm, field_ref),
            (basis_hbm, basis_ref),
            (list_hbm, list_ref),
            (top_hbm, top_ref),
        ],
        sem,
    )
    device = lax.axis_index("dev")
    place_ref[0] = (lax.axis_index("group") * lax.axis_size("dev") + device) * leaves
    place_ref[1] = device % 2
    copies[0].wait()
    for j in range(rank // 2):
        rows_ref[j * leaves : (j + 1) * leaves] = transfer_ref[:, j * lanes : (j + 1) * lanes].astype(jnp.float32)
    for i in range(leaves):
        rows = rows_ref[pl.ds(i, rank // 2, stride=leaves), :]
        emat_ref[i, pl.ds(0, rank // 2, stride=2), :] = rows
        emat_ref[i, pl.ds(1, rank // 2, stride=2), :] = pltpu.roll(rows, rank, 1)
    copies[1].wait()
    copies[2].wait()
    cells = split(field_ref[...])
    folds = []
    for c in range(clusters):
        tiles = []
        for i in range(c * LEAF_CL, (c + 1) * LEAF_CL):
            emat = emat_ref[i][:, :rank].astype(jnp.bfloat16)
            fold = lax.dot_general(
                emat, basis_ref[i], (((0,), (0,)), ((), ())), preferred_element_type=jnp.float32
            )
            tiles.append(fold.astype(jnp.bfloat16))
        folds.append(jnp.concatenate(tiles, axis=1))
    parts = [halves_sum(dot_tt(cells[:, c * span : (c + 1) * span], fold)) for c, fold in enumerate(folds)]
    sent = send_chunk(chunk_hbm, chunk_ref, chunk_sem, parts)
    for c, fold in enumerate(folds):
        fold_ref[c] = fold
    put_halo(device % 2, field_ref, inner_ref, outer_ref)
    copies[3].wait()
    copies[4].wait()
    sent.wait()


def prepare_kernel(
    place_ref, list_ref, top_ref, field_ref, fold_ref, coupling_hbm, blocks_hbm,
    near_ref, ends_ref, smat_ref, turned_ref, gram_ref, table, blocks_ref, coupling_ref, rows_ref, sem
):
    pairs, each = part_copies(blocks_hbm, blocks_ref)
    copies = load_all([(coupling_hbm, coupling_ref)] + pairs, sem)
    clusters, rank, span = fold_ref.shape
    half = rank // 2
    row = lax.broadcasted_iota(jnp.int32, (rank, rank), 0)
    column = lax.broadcasted_iota(jnp.int32, (rank, rank), 1)
    order = (column == 2 * (row % half) + row // half).astype(jnp.bfloat16)
    for c in range(clusters):
        turned = dot_nn(order, fold_ref[c]).astype(jnp.bfloat16)
        turned_ref[c] = turned
        gram_ref[c] = dot_tt(turned, fold_ref[c]).astype(jnp.bfloat16)
    copies[0].wait()
    lower = lax.broadcasted_iota(jnp.int32, (half, 2 * rank), 1) < rank
    for c in range(clusters):
        for j in range(half):
            rows_ref[j * TOPK : (j + 1) * TOPK] = coupling_ref[c, :, j * 2 * rank : (j + 1) * 2 * rank].astype(jnp.float32)
        for k in range(TOPK):
            rows = rows_ref[pl.ds(k, half, stride=TOPK), :]
            upper = jnp.broadcast_to(top_ref[c, k] % 2, lower.shape) == 1
            here = lower != upper
            turned = pltpu.roll(rows, rank, 1)
            even = jnp.where(here, jnp.where(upper, turned, rows), 0.0)
            odd = jnp.where(here, jnp.where(upper, rows, turned), 0.0)
            at = slice(k * 2 * rank, (k + 1) * 2 * rank)
            smat_ref[c, :, at] = jnp.concatenate([even, odd], axis=0).astype(jnp.bfloat16)
    ready = wait_parts(copies[1:], each)
    near_sum(place_ref, list_ref, field_ref, blocks_ref, near_ref, ends_ref, table, ready)


def halves_sum(total):
    rhs = total.shape[0] // 2
    return total[:rhs] + total[rhs:]


def near_sum(place_ref, list_ref, field_ref, blocks_ref, near_ref, ends_ref, table, ready):
    leaves, _, leaf, _ = blocks_ref.shape
    for i in range(leaves):
        table[i] = split(field_ref[:, i * leaf : (i + 1) * leaf])
    table[leaves] = jnp.zeros(table.shape[1:], table.dtype)
    first = place_ref[0]
    for i in range(leaves):
        ready(min(i + HALO, leaves - 1))
        values, blocks = [], []
        for k in range(NEAR):
            at = list_ref[k, i] - first
            inside = (at >= 0) & (at < leaves)
            values.append(table[jnp.where(inside, at, leaves)])
            blocks.append(blocks_ref[jnp.where(inside, at, i), k])
        total = dot_nn(jnp.concatenate(values, axis=1), jnp.concatenate(blocks, axis=0))
        near_ref[:, i * leaf : (i + 1) * leaf] = halves_sum(total)
    ends_ref[:HALO] = blocks_ref[:HALO]
    ends_ref[HALO:] = blocks_ref[leaves - HALO :]


def wait_parts(copies, each):
    done = []

    def ready(leaf):
        while len(done) <= leaf // each:
            copies[len(done)].wait()
            done.append(leaf)

    return ready


def part_copies(blocks_hbm, blocks_ref):
    each = blocks_ref.shape[0] // PARTS
    spans = [pl.ds(at * each, each) for at in range(PARTS)]
    return [(blocks_hbm.at[at], blocks_ref.at[at]) for at in spans], each


def near_kernel(
    place_ref, list_ref, field_ref, blocks_hbm, near_ref, ends_ref, table, blocks_ref, sem
):
    pairs, each = part_copies(blocks_hbm, blocks_ref)
    ready = wait_parts(load_all(pairs, sem), each)
    near_sum(place_ref, list_ref, field_ref, blocks_ref, near_ref, ends_ref, table, ready)


def edge_kernel(leaves, place_ref, list_ref, inner_ref, outer_ref, ends_ref, edge_ref, table):
    leaf = ends_ref.shape[2]
    zero = 2 * HALO
    table[zero] = jnp.zeros(table.shape[1:], table.dtype)
    even = jnp.where(place_ref[1] == 0, HALO, 0)
    for i in range(HALO):
        table[even + i] = inner_ref[:, i * leaf : (i + 1) * leaf]
        table[HALO - even + i] = outer_ref[:, i * leaf : (i + 1) * leaf]
    first = place_ref[0]
    for i in range(2 * HALO):
        own = i if i < HALO else leaves - 2 * HALO + i

        def pick(k):
            at = list_ref[k, own] - first
            return table[jnp.where(at < 0, at + HALO, jnp.where(at >= leaves, at - leaves + HALO, zero))]

        values = jnp.concatenate([pick(k) for k in range(NEAR)], axis=1)
        blocks = jnp.concatenate([ends_ref[i, k] for k in range(NEAR)], axis=1)
        edge_ref[:, i * leaf : (i + 1) * leaf] = halves_sum(dot_tt(values, blocks))


def near_part(c, clusters, near_ref, edge_ref):
    span = near_ref.shape[1] // clusters
    near = near_ref[:, c * span : (c + 1) * span]
    half = edge_ref.shape[1] // 2
    rest = jnp.zeros((near.shape[0], span - half), jnp.float32)
    if c == 0:
        near += jnp.concatenate([edge_ref[:, :half], rest], axis=1)
    if c == clusters - 1:
        near += jnp.concatenate([rest, edge_ref[:, half:]], axis=1)
    return near


def down_parts(top_ref, table_ref, smat_ref):
    downs = []
    for c in range(smat_ref.shape[0]):
        tiles = [table_ref[top_ref[c, k] >> 1] for k in range(TOPK)]
        downs.append(dot_tt(jnp.concatenate(tiles, axis=1), smat_ref[c]).astype(jnp.bfloat16))
    return downs


def second_kernel(
    place_ref, top_ref, table_ref, smat_ref, turned_ref, gram_ref, fold_ref, nugget_ref, field_ref, near_ref, edge_ref,
    chunk_hbm, image_ref, inner_ref, outer_ref, chunk_ref, sem,
):
    clusters, _, span = fold_ref.shape
    spans = [slice(c * span, (c + 1) * span) for c in range(clusters)]
    downs = down_parts(top_ref, table_ref, smat_ref)
    bases, parts = [], []
    for c, at in enumerate(spans):
        bases.append(nugget_ref[:, at] * field_ref[:, at] + near_part(c, clusters, near_ref, edge_ref))
        parts.append(halves_sum(dot_tt(split(bases[c]), fold_ref[c])))
    parts = [part + dot_nn(down, gram_ref[c]) for c, (part, down) in enumerate(zip(parts, downs))]
    sent = send_chunk(chunk_hbm, chunk_ref, sem, parts)
    for c, at in enumerate(spans):
        image_ref[:, at] = bases[c] + dot_nn(downs[c], turned_ref[c])
    put_halo(place_ref[1], image_ref, inner_ref, outer_ref)
    sent.wait()


def third_kernel(
    top_ref, table_ref, smat_ref, turned_ref, nugget_ref, field_ref, image_ref, near_ref, edge_ref,
    twice_ref, sums_ref,
):
    clusters, _, span = turned_ref.shape
    rhs = field_ref.shape[0]
    for c, down in enumerate(down_parts(top_ref, table_ref, smat_ref)):
        at = slice(c * span, (c + 1) * span)
        far = dot_nn(down, turned_ref[c])
        near = near_part(c, clusters, near_ref, edge_ref)
        twice_ref[:, at] = nugget_ref[:, at] * image_ref[:, at] + near + far

    def dot(left, right):
        return jnp.sum(left * right, axis=1, keepdims=True)

    field, image, twice = field_ref[...], image_ref[...], twice_ref[...]
    size = dot(image, image)
    cross = dot(field, image)
    own = cross / jnp.where(size > 0, size, 1.0)
    rest = field - own * image
    bent = image - own * twice
    sums = [
        dot(field, field),
        cross,
        size,
        dot(rest, rest),
        dot(rest, bent),
        dot(image, bent) + dot(rest, twice),
        dot(image, twice),
    ]
    width = sums_ref.shape[2]
    lane = lax.broadcasted_iota(jnp.int32, (rhs, width), 1)
    row = lax.broadcasted_iota(jnp.int32, (rhs, width), 0)
    packed = jnp.zeros((rhs, width), jnp.float32)
    for at, value in enumerate(sums):
        packed = jnp.where(lane == row + at * rhs, value, packed)
    flat = jnp.sum(packed, axis=0, keepdims=True)
    sums_ref[...] = jnp.broadcast_to(flat[None], sums_ref.shape)


def last_kernel(sums_ref, field_ref, image_ref, twice_ref, solution_ref, residual_ref):
    rhs = field_ref.shape[0]
    sums = sums_ref[...].reshape(sums_ref.shape[0], sums_ref.shape[2]).T

    def part(at):
        return sums[at * rhs : (at + 1) * rhs]

    def total(value):
        return jnp.sum(value, axis=1, keepdims=True)

    norm = total(part(0))
    curve = total(part(1))
    size = part(2)
    own = part(1) / jnp.where(size > 0, size, 1.0)
    alpha = norm / curve
    delta = own - alpha
    norm_next = total(part(3) + delta * delta * size)
    rest_bent = total(part(4) + delta * (part(5) + delta * part(6)))
    rest_image = total(delta * size)
    beta = norm_next / norm
    curve_next = rest_bent + beta * (2.0 * rest_image + beta * curve)
    alpha_next = norm_next / curve_next
    outer = alpha + alpha_next * (1.0 + beta)
    inner = alpha * alpha_next
    field, image = field_ref[...], image_ref[...]
    solution_ref[...] = outer * field - inner * image
    residual_ref[...] = field - outer * image + inner * twice_ref[...]


def exchange(chunk):
    return lax.all_to_all(chunk, AXES, 0, 0)


def swap_cores(value):
    return lax.ppermute(value, "dev", [(i, i ^ 1) for i in range(lax.axis_size("dev"))])


def swap_ends(inner, outer):
    count = lax.axis_size("dev")
    inner = swap_cores(inner)
    pairs = [(i, i + 1) for i in range(1, count - 1, 2)]
    outer = lax.ppermute(outer, "dev", pairs + [(b, a) for a, b in pairs])
    return inner, outer


def per_device(right_side, nugget, near_blocks, near_list, basis, transfer, coupling, top_list):
    rhs, width = right_side.shape
    leaves, rank, leaf = basis.shape
    clusters = coupling.shape[0]
    span = leaf * LEAF_CL
    devices = lax.axis_size("group") * lax.axis_size("dev")
    nugget = nugget[None]
    chunk_shape = pltpu.HBM((devices, clusters // 2, rhs, 2 * rank), jnp.bfloat16)
    chunk_scratch = [pltpu.VMEM(chunk_shape.shape, jnp.bfloat16), pltpu.SemaphoreType.DMA((1,))]
    end = HALO * leaf
    field_shape = pltpu.VMEM((rhs, width), jnp.float32)
    fold_shape = pltpu.VMEM((clusters, rank, span), jnp.bfloat16)
    end_shape = pltpu.VMEM((2 * rhs, end), jnp.bfloat16)

    chunk, field, fold, inner, outer, place, near_list, top_list = pl.pallas_call(
        first_kernel,
        in_specs=[HBM] * 5,
        out_specs=[HBM] + [VMEM] * 4 + [SMEM] * 3,
        out_shape=[
            chunk_shape,
            field_shape,
            fold_shape,
            end_shape,
            end_shape,
            pltpu.SMEM((2,), jnp.int32),
            pltpu.SMEM(near_list.T.shape, near_list.dtype),
            pltpu.SMEM(top_list.shape, top_list.dtype),
        ],
        scratch_shapes=chunk_scratch
        + [
            pltpu.VMEM(basis.shape, basis.dtype),
            pltpu.VMEM(transfer.shape, transfer.dtype),
            pltpu.VMEM((leaves * rank // 2, 2 * rank), jnp.float32),
            pltpu.VMEM((leaves, rank, 2 * rank), jnp.float32),
            pltpu.SemaphoreType.DMA((5,)),
        ],
        compiler_params=PARAMS,
        name="first",
    )(*in_hbm(right_side, basis, transfer, near_list.T, top_list))
    table = exchange(chunk).reshape(-1, rhs, 2 * rank)
    ends_shape = pltpu.VMEM((2 * HALO,) + near_blocks.shape[1:], near_blocks.dtype)
    near_scratch = [
        pltpu.VMEM((leaves + 1, 2 * rhs, leaf), jnp.bfloat16),
        pltpu.VMEM(near_blocks.shape, near_blocks.dtype),
    ]

    def edge_product(inner, outer, ends):
        return pl.pallas_call(
            functools.partial(edge_kernel, leaves),
            in_specs=[SMEM] * 2 + [VMEM] * 3,
            out_specs=VMEM,
            out_shape=pltpu.VMEM((rhs, 2 * end), jnp.float32),
            scratch_shapes=[pltpu.VMEM((2 * HALO + 1, 2 * rhs, leaf), jnp.bfloat16)],
            compiler_params=PARAMS,
            name="edge",
        )(place, near_list, *swap_ends(inner, outer), ends)

    near, ends, smat, turned, gram = pl.pallas_call(
        prepare_kernel,
        in_specs=[SMEM] * 3 + [VMEM] * 2 + [HBM] * 2,
        out_specs=[VMEM] * 5,
        out_shape=[
            field_shape,
            ends_shape,
            pltpu.VMEM((clusters, rank, TOPK * 2 * rank), jnp.bfloat16),
            fold_shape,
            pltpu.VMEM((clusters, rank, rank), jnp.bfloat16),
        ],
        scratch_shapes=near_scratch
        + [
            pltpu.VMEM(coupling.shape, coupling.dtype),
            pltpu.VMEM((rank // 2 * TOPK, 2 * rank), jnp.float32),
            pltpu.SemaphoreType.DMA((1 + PARTS,)),
        ],
        compiler_params=PARAMS,
        name="prepare",
    )(place, near_list, top_list, field, fold, *in_hbm(coupling, near_blocks))
    edge = edge_product(inner, outer, ends)

    chunk, image, inner, outer = pl.pallas_call(
        second_kernel,
        in_specs=[SMEM] * 2 + [VMEM] * 9,
        out_specs=[HBM] + [VMEM] * 3,
        out_shape=[chunk_shape, field_shape, end_shape, end_shape],
        scratch_shapes=chunk_scratch,
        compiler_params=PARAMS,
        name="second",
    )(place, top_list, table, smat, turned, gram, fold, nugget, field, near, edge)
    table = exchange(chunk).reshape(-1, rhs, 2 * rank)
    near, ends = pl.pallas_call(
        near_kernel,
        in_specs=[SMEM] * 2 + [VMEM, HBM],
        out_specs=[VMEM] * 2,
        out_shape=[field_shape, ends_shape],
        scratch_shapes=near_scratch + [pltpu.SemaphoreType.DMA((PARTS,))],
        compiler_params=PARAMS,
        name="near",
    )(place, near_list, image, *in_hbm(near_blocks))
    edge = edge_product(inner, outer, ends)

    twice, sums = pl.pallas_call(
        third_kernel,
        in_specs=[SMEM] + [VMEM] * 8,
        out_specs=[VMEM] * 2,
        out_shape=[field_shape, struct((devices, 1, 8 * rhs), jnp.float32)],
        compiler_params=PARAMS,
        name="third",
    )(top_list, table, smat, turned, nugget, field, image, near, edge)
    sums = exchange(sums)

    return pl.pallas_call(
        last_kernel,
        in_specs=[VMEM] * 4,
        out_specs=[VMEM] * 2,
        out_shape=[struct((rhs, width), jnp.float32)] * 2,
        compiler_params=PARAMS,
        name="last",
    )(sums, field, image, twice)


def solution(mesh):
    placed = (
        P(None, AXES),
        P(AXES),
        P(AXES, None, None, None),
        P(AXES, None),
        P(AXES, None, None),
        P(AXES, None),
        P(AXES, None, None),
        P(AXES, None),
    )
    return jax.shard_map(
        per_device,
        mesh=mesh,
        in_specs=placed,
        out_specs=(P(None, AXES), P(None, AXES)),
        check_vma=False,
    )
```

```python
import functools

import jax
import jax.numpy as jnp
from jax import lax
from jax.experimental import pallas as pl
from jax.experimental.pallas import tpu as pltpu
from jax.sharding import PartitionSpec as P

LEAF_CL = 8
TOPK = 16
NEAR = 4
PARTS = 4
HALO = 4
AXES = ("group", "dev")
VMEM = pl.BlockSpec(memory_space=pltpu.VMEM)
SMEM = pl.BlockSpec(memory_space=pltpu.SMEM)
HBM = pl.BlockSpec(memory_space=pltpu.HBM)
PARAMS = pltpu.CompilerParams(vmem_limit_bytes=16 * 1024 * 1024)


def struct(shape, dtype):
    return jax.ShapeDtypeStruct(shape, dtype)


def in_hbm(*values):
    return [pltpu.with_memory_space_constraint(value, pltpu.HBM) for value in values]


def load_all(pairs, sem):
    copies = [pltpu.make_async_copy(src, dst, sem.at[at]) for at, (src, dst) in enumerate(pairs)]
    for copy in copies:
        copy.start()
    return copies


def dot_tt(left, right):
    return lax.dot_general(
        left, right, (((1,), (1,)), ((), ())), preferred_element_type=jnp.float32
    )


def dot_nn(left, right):
    return lax.dot_general(
        left, right, (((1,), (0,)), ((), ())), preferred_element_type=jnp.float32
    )


def split(value):
    high = value.astype(jnp.bfloat16)
    low = (value - high.astype(jnp.float32)).astype(jnp.bfloat16)
    return jnp.concatenate([high, low], axis=0)


def send_chunk(chunk_hbm, chunk_ref, sem, parts):
    for at in range(len(parts) // 2):
        pair = jnp.concatenate(parts[2 * at : 2 * at + 2], axis=1).astype(jnp.bfloat16)
        chunk_ref[:, at] = jnp.broadcast_to(pair[None], (chunk_ref.shape[0],) + pair.shape)
    copy = pltpu.make_async_copy(chunk_ref, chunk_hbm, sem.at[0])
    copy.start()
    return copy


def put_halo(core, field_ref, inner_ref, outer_ref):
    span = inner_ref.shape[1]
    head, tail = split(field_ref[:, :span]), split(field_ref[:, field_ref.shape[1] - span :])

    @pl.when(core == 0)
    def _():
        inner_ref[...] = tail
        outer_ref[...] = head

    @pl.when(core != 0)
    def _():
        inner_ref[...] = head
        outer_ref[...] = tail


def first_kernel(
    field_hbm, basis_hbm, transfer_hbm, list_hbm, top_hbm,
    chunk_hbm, field_ref, fold_ref, inner_ref, outer_ref, place_ref, list_ref, top_ref,
    chunk_ref, chunk_sem, basis_ref, transfer_ref, rows_ref, emat_ref, sem,
):
    clusters, rank, span = fold_ref.shape
    leaves, _, leaf = basis_ref.shape
    rhs = field_ref.shape[0]
    lanes = 2 * rank
    copies = load_all(
        [
            (transfer_hbm, transfer_ref),
            (field_hbm, field_ref),
            (basis_hbm, basis_ref),
            (list_hbm, list_ref),
            (top_hbm, top_ref),
        ],
        sem,
    )
    device = lax.axis_index("dev")
    place_ref[0] = (lax.axis_index("group") * lax.axis_size("dev") + device) * leaves
    place_ref[1] = device % 2
    copies[0].wait()
    for j in range(rank // 2):
        rows_ref[j * leaves : (j + 1) * leaves] = transfer_ref[:, j * lanes : (j + 1) * lanes].astype(jnp.float32)
    for i in range(leaves):
        rows = rows_ref[pl.ds(i, rank // 2, stride=leaves), :]
        emat_ref[i, pl.ds(0, rank // 2, stride=2), :] = rows
        emat_ref[i, pl.ds(1, rank // 2, stride=2), :] = pltpu.roll(rows, rank, 1)
    copies[1].wait()
    copies[2].wait()
    cells = split(field_ref[...])
    folds = []
    for c in range(clusters):
        tiles = []
        for i in range(c * LEAF_CL, (c + 1) * LEAF_CL):
            emat = emat_ref[i][:, :rank].astype(jnp.bfloat16)
            fold = lax.dot_general(
                emat, basis_ref[i], (((0,), (0,)), ((), ())), preferred_element_type=jnp.float32
            )
            tiles.append(fold.astype(jnp.bfloat16))
        folds.append(jnp.concatenate(tiles, axis=1))
    parts = [halves_sum(dot_tt(cells[:, c * span : (c + 1) * span], fold)) for c, fold in enumerate(folds)]
    sent = send_chunk(chunk_hbm, chunk_ref, chunk_sem, parts)
    for c, fold in enumerate(folds):
        fold_ref[c] = fold
    put_halo(device % 2, field_ref, inner_ref, outer_ref)
    copies[3].wait()
    copies[4].wait()
    sent.wait()


def prepare_kernel(
    place_ref, list_ref, field_ref, fold_ref, coupling_hbm, blocks_hbm,
    near_ref, ends_ref, smat_ref, turned_ref, gram_ref, table, blocks_ref, coupling_ref, rows_ref, sem
):
    pairs, each = part_copies(blocks_hbm, blocks_ref)
    copies = load_all([(coupling_hbm, coupling_ref)] + pairs, sem)
    clusters, rank, span = fold_ref.shape
    half = rank // 2
    row = lax.broadcasted_iota(jnp.int32, (rank, rank), 0)
    column = lax.broadcasted_iota(jnp.int32, (rank, rank), 1)
    order = (column == 2 * (row % half) + row // half).astype(jnp.bfloat16)
    for c in range(clusters):
        turned = dot_nn(order, fold_ref[c]).astype(jnp.bfloat16)
        turned_ref[c] = turned
        gram_ref[c] = dot_tt(turned, fold_ref[c]).astype(jnp.bfloat16)
    copies[0].wait()
    lower = lax.broadcasted_iota(jnp.int32, (half, 2 * rank), 1) < rank
    for c in range(clusters):
        for j in range(half):
            rows_ref[j * TOPK : (j + 1) * TOPK] = coupling_ref[c, :, j * 2 * rank : (j + 1) * 2 * rank].astype(jnp.float32)
        for k in range(0, TOPK, 2):
            one = rows_ref[pl.ds(k, half, stride=TOPK), :]
            two = rows_ref[pl.ds(k + 1, half, stride=TOPK), :]
            even = jnp.where(lower, one, pltpu.roll(two, rank, 1))
            odd = jnp.where(lower, pltpu.roll(one, rank, 1), two)
            smat_ref[c, :, k * rank : (k + 2) * rank] = jnp.concatenate([even, odd], axis=0).astype(jnp.bfloat16)
    ready = wait_parts(copies[1:], each)
    near_sum(place_ref, list_ref, field_ref, blocks_ref, near_ref, ends_ref, table, ready)


def halves_sum(total):
    rhs = total.shape[0] // 2
    return total[:rhs] + total[rhs:]


def near_sum(place_ref, list_ref, field_ref, blocks_ref, near_ref, ends_ref, table, ready):
    leaves, _, leaf, _ = blocks_ref.shape
    for i in range(leaves):
        table[i] = split(field_ref[:, i * leaf : (i + 1) * leaf])
    table[leaves] = jnp.zeros(table.shape[1:], table.dtype)
    first = place_ref[0]
    for i in range(leaves):
        ready(min(i + HALO, leaves - 1))
        values, blocks = [], []
        for k in range(NEAR):
            at = list_ref[k, i] - first
            inside = (at >= 0) & (at < leaves)
            values.append(table[jnp.where(inside, at, leaves)])
            blocks.append(blocks_ref[jnp.where(inside, at, i), k])
        total = dot_nn(jnp.concatenate(values, axis=1), jnp.concatenate(blocks, axis=0))
        near_ref[:, i * leaf : (i + 1) * leaf] = halves_sum(total)
    ends_ref[:HALO] = blocks_ref[:HALO]
    ends_ref[HALO:] = blocks_ref[leaves - HALO :]


def wait_parts(copies, each):
    done = []

    def ready(leaf):
        while len(done) <= leaf // each:
            copies[len(done)].wait()
            done.append(leaf)

    return ready


def part_copies(blocks_hbm, blocks_ref):
    each = blocks_ref.shape[0] // PARTS
    spans = [pl.ds(at * each, each) for at in range(PARTS)]
    return [(blocks_hbm.at[at], blocks_ref.at[at]) for at in spans], each


def near_kernel(
    place_ref, list_ref, field_ref, blocks_hbm, near_ref, ends_ref, table, blocks_ref, sem
):
    pairs, each = part_copies(blocks_hbm, blocks_ref)
    ready = wait_parts(load_all(pairs, sem), each)
    near_sum(place_ref, list_ref, field_ref, blocks_ref, near_ref, ends_ref, table, ready)


def edge_kernel(leaves, place_ref, list_ref, inner_ref, outer_ref, ends_ref, edge_ref, table):
    leaf = ends_ref.shape[2]
    zero = 2 * HALO
    table[zero] = jnp.zeros(table.shape[1:], table.dtype)
    even = jnp.where(place_ref[1] == 0, HALO, 0)
    for i in range(HALO):
        table[even + i] = inner_ref[:, i * leaf : (i + 1) * leaf]
        table[HALO - even + i] = outer_ref[:, i * leaf : (i + 1) * leaf]
    first = place_ref[0]
    for i in range(2 * HALO):
        own = i if i < HALO else leaves - 2 * HALO + i

        def pick(k):
            at = list_ref[k, own] - first
            return table[jnp.where(at < 0, at + HALO, jnp.where(at >= leaves, at - leaves + HALO, zero))]

        values = jnp.concatenate([pick(k) for k in range(NEAR)], axis=1)
        blocks = jnp.concatenate([ends_ref[i, k] for k in range(NEAR)], axis=1)
        edge_ref[:, i * leaf : (i + 1) * leaf] = halves_sum(dot_tt(values, blocks))


def near_part(c, clusters, near_ref, edge_ref):
    span = near_ref.shape[1] // clusters
    near = near_ref[:, c * span : (c + 1) * span]
    half = edge_ref.shape[1] // 2
    rest = jnp.zeros((near.shape[0], span - half), jnp.float32)
    if c == 0:
        near += jnp.concatenate([edge_ref[:, :half], rest], axis=1)
    if c == clusters - 1:
        near += jnp.concatenate([rest, edge_ref[:, half:]], axis=1)
    return near


def down_parts(top_ref, table_ref, smat_ref):
    shape = table_ref.shape[1:]
    rank = shape[1] // 2
    lower = lax.broadcasted_iota(jnp.int32, shape, 1) < rank

    def pick(c, k):
        top = top_ref[c, k]
        tile = table_ref[top >> 1]
        turned = jnp.concatenate([tile[:, rank:], tile[:, :rank]], axis=1)
        return jnp.where(jnp.broadcast_to(top & 1, shape) == k % 2, tile, turned)

    downs = []
    for c in range(smat_ref.shape[0]):
        tiles = [jnp.where(lower, pick(c, k), pick(c, k + 1)) for k in range(0, TOPK, 2)]
        downs.append(dot_tt(jnp.concatenate(tiles, axis=1), smat_ref[c]).astype(jnp.bfloat16))
    return downs


def second_kernel(
    place_ref, top_ref, table_ref, smat_ref, turned_ref, gram_ref, fold_ref, nugget_ref, field_ref, near_ref, edge_ref,
    chunk_hbm, image_ref, inner_ref, outer_ref, chunk_ref, sem,
):
    clusters, _, span = fold_ref.shape
    spans = [slice(c * span, (c + 1) * span) for c in range(clusters)]
    downs = down_parts(top_ref, table_ref, smat_ref)
    bases, parts = [], []
    for c, at in enumerate(spans):
        bases.append(nugget_ref[:, at] * field_ref[:, at] + near_part(c, clusters, near_ref, edge_ref))
        parts.append(halves_sum(dot_tt(split(bases[c]), fold_ref[c])))
    parts = [part + dot_nn(down, gram_ref[c]) for c, (part, down) in enumerate(zip(parts, downs))]
    sent = send_chunk(chunk_hbm, chunk_ref, sem, parts)
    for c, at in enumerate(spans):
        image_ref[:, at] = bases[c] + dot_nn(downs[c], turned_ref[c])
    put_halo(place_ref[1], image_ref, inner_ref, outer_ref)
    sent.wait()


def third_kernel(
    top_ref, table_ref, smat_ref, turned_ref, nugget_ref, field_ref, image_ref, near_ref, edge_ref,
    twice_ref, sums_ref,
):
    clusters, _, span = turned_ref.shape
    rhs = field_ref.shape[0]
    for c, down in enumerate(down_parts(top_ref, table_ref, smat_ref)):
        at = slice(c * span, (c + 1) * span)
        far = dot_nn(down, turned_ref[c])
        near = near_part(c, clusters, near_ref, edge_ref)
        twice_ref[:, at] = nugget_ref[:, at] * image_ref[:, at] + near + far

    def dot(left, right):
        return jnp.sum(left * right, axis=1, keepdims=True)

    field, image, twice = field_ref[...], image_ref[...], twice_ref[...]
    size = dot(image, image)
    cross = dot(field, image)
    own = cross / jnp.where(size > 0, size, 1.0)
    rest = field - own * image
    bent = image - own * twice
    sums = [
        dot(field, field),
        cross,
        size,
        dot(rest, rest),
        dot(rest, bent),
        dot(image, bent) + dot(rest, twice),
        dot(image, twice),
    ]
    width = sums_ref.shape[2]
    lane = lax.broadcasted_iota(jnp.int32, (rhs, width), 1)
    row = lax.broadcasted_iota(jnp.int32, (rhs, width), 0)
    packed = jnp.zeros((rhs, width), jnp.float32)
    for at, value in enumerate(sums):
        packed = jnp.where(lane == row + at * rhs, value, packed)
    flat = jnp.sum(packed, axis=0, keepdims=True)
    sums_ref[...] = jnp.broadcast_to(flat[None], sums_ref.shape)


def last_kernel(sums_ref, field_ref, image_ref, twice_ref, solution_ref, residual_ref):
    rhs = field_ref.shape[0]
    sums = sums_ref[...].reshape(sums_ref.shape[0], sums_ref.shape[2]).T

    def part(at):
        return sums[at * rhs : (at + 1) * rhs]

    def total(value):
        return jnp.sum(value, axis=1, keepdims=True)

    norm = total(part(0))
    curve = total(part(1))
    size = part(2)
    own = part(1) / jnp.where(size > 0, size, 1.0)
    alpha = norm / curve
    delta = own - alpha
    norm_next = total(part(3) + delta * delta * size)
    rest_bent = total(part(4) + delta * (part(5) + delta * part(6)))
    rest_image = total(delta * size)
    beta = norm_next / norm
    curve_next = rest_bent + beta * (2.0 * rest_image + beta * curve)
    alpha_next = norm_next / curve_next
    outer = alpha + alpha_next * (1.0 + beta)
    inner = alpha * alpha_next
    field, image = field_ref[...], image_ref[...]
    solution_ref[...] = outer * field - inner * image
    residual_ref[...] = field - outer * image + inner * twice_ref[...]


def exchange(chunk):
    return lax.all_to_all(chunk, AXES, 0, 0)


def swap_cores(value):
    return lax.ppermute(value, "dev", [(i, i ^ 1) for i in range(lax.axis_size("dev"))])


def swap_ends(inner, outer):
    count = lax.axis_size("dev")
    inner = swap_cores(inner)
    pairs = [(i, i + 1) for i in range(1, count - 1, 2)]
    outer = lax.ppermute(outer, "dev", pairs + [(b, a) for a, b in pairs])
    return inner, outer


def per_device(right_side, nugget, near_blocks, near_list, basis, transfer, coupling, top_list):
    rhs, width = right_side.shape
    leaves, rank, leaf = basis.shape
    clusters = coupling.shape[0]
    span = leaf * LEAF_CL
    devices = lax.axis_size("group") * lax.axis_size("dev")
    nugget = nugget[None]
    chunk_shape = pltpu.HBM((devices, clusters // 2, rhs, 2 * rank), jnp.bfloat16)
    chunk_scratch = [pltpu.VMEM(chunk_shape.shape, jnp.bfloat16), pltpu.SemaphoreType.DMA((1,))]
    end = HALO * leaf
    field_shape = pltpu.VMEM((rhs, width), jnp.float32)
    fold_shape = pltpu.VMEM((clusters, rank, span), jnp.bfloat16)
    end_shape = pltpu.VMEM((2 * rhs, end), jnp.bfloat16)

    chunk, field, fold, inner, outer, place, near_list, top_list = pl.pallas_call(
        first_kernel,
        in_specs=[HBM] * 5,
        out_specs=[HBM] + [VMEM] * 4 + [SMEM] * 3,
        out_shape=[
            chunk_shape,
            field_shape,
            fold_shape,
            end_shape,
            end_shape,
            pltpu.SMEM((2,), jnp.int32),
            pltpu.SMEM(near_list.T.shape, near_list.dtype),
            pltpu.SMEM(top_list.shape, top_list.dtype),
        ],
        scratch_shapes=chunk_scratch
        + [
            pltpu.VMEM(basis.shape, basis.dtype),
            pltpu.VMEM(transfer.shape, transfer.dtype),
            pltpu.VMEM((leaves * rank // 2, 2 * rank), jnp.float32),
            pltpu.VMEM((leaves, rank, 2 * rank), jnp.float32),
            pltpu.SemaphoreType.DMA((5,)),
        ],
        compiler_params=PARAMS,
        name="first",
    )(*in_hbm(right_side, basis, transfer, near_list.T, top_list))
    table = exchange(chunk).reshape(-1, rhs, 2 * rank)
    ends_shape = pltpu.VMEM((2 * HALO,) + near_blocks.shape[1:], near_blocks.dtype)
    near_scratch = [
        pltpu.VMEM((leaves + 1, 2 * rhs, leaf), jnp.bfloat16),
        pltpu.VMEM(near_blocks.shape, near_blocks.dtype),
    ]

    def edge_product(inner, outer, ends):
        return pl.pallas_call(
            functools.partial(edge_kernel, leaves),
            in_specs=[SMEM] * 2 + [VMEM] * 3,
            out_specs=VMEM,
            out_shape=pltpu.VMEM((rhs, 2 * end), jnp.float32),
            scratch_shapes=[pltpu.VMEM((2 * HALO + 1, 2 * rhs, leaf), jnp.bfloat16)],
            compiler_params=PARAMS,
            name="edge",
        )(place, near_list, *swap_ends(inner, outer), ends)

    near, ends, smat, turned, gram = pl.pallas_call(
        prepare_kernel,
        in_specs=[SMEM] * 2 + [VMEM] * 2 + [HBM] * 2,
        out_specs=[VMEM] * 5,
        out_shape=[
            field_shape,
            ends_shape,
            pltpu.VMEM((clusters, rank, TOPK * rank), jnp.bfloat16),
            fold_shape,
            pltpu.VMEM((clusters, rank, rank), jnp.bfloat16),
        ],
        scratch_shapes=near_scratch
        + [
            pltpu.VMEM(coupling.shape, coupling.dtype),
            pltpu.VMEM((rank // 2 * TOPK, 2 * rank), jnp.float32),
            pltpu.SemaphoreType.DMA((1 + PARTS,)),
        ],
        compiler_params=PARAMS,
        name="prepare",
    )(place, near_list, field, fold, *in_hbm(coupling, near_blocks))
    edge = edge_product(inner, outer, ends)

    chunk, image, inner, outer = pl.pallas_call(
        second_kernel,
        in_specs=[SMEM] * 2 + [VMEM] * 9,
        out_specs=[HBM] + [VMEM] * 3,
        out_shape=[chunk_shape, field_shape, end_shape, end_shape],
        scratch_shapes=chunk_scratch,
        compiler_params=PARAMS,
        name="second",
    )(place, top_list, table, smat, turned, gram, fold, nugget, field, near, edge)
    table = exchange(chunk).reshape(-1, rhs, 2 * rank)
    near, ends = pl.pallas_call(
        near_kernel,
        in_specs=[SMEM] * 2 + [VMEM, HBM],
        out_specs=[VMEM] * 2,
        out_shape=[field_shape, ends_shape],
        scratch_shapes=near_scratch + [pltpu.SemaphoreType.DMA((PARTS,))],
        compiler_params=PARAMS,
        name="near",
    )(place, near_list, image, *in_hbm(near_blocks))
    edge = edge_product(inner, outer, ends)

    twice, sums = pl.pallas_call(
        third_kernel,
        in_specs=[SMEM] + [VMEM] * 8,
        out_specs=[VMEM] * 2,
        out_shape=[field_shape, struct((devices, 1, 8 * rhs), jnp.float32)],
        compiler_params=PARAMS,
        name="third",
    )(top_list, table, smat, turned, nugget, field, image, near, edge)
    sums = exchange(sums)

    return pl.pallas_call(
        last_kernel,
        in_specs=[VMEM] * 4,
        out_specs=[VMEM] * 2,
        out_shape=[struct((rhs, width), jnp.float32)] * 2,
        compiler_params=PARAMS,
        name="last",
    )(sums, field, image, twice)


def solution(mesh):
    placed = (
        P(None, AXES),
        P(AXES),
        P(AXES, None, None, None),
        P(AXES, None),
        P(AXES, None, None),
        P(AXES, None),
        P(AXES, None, None),
        P(AXES, None),
    )
    return jax.shard_map(
        per_device,
        mesh=mesh,
        in_specs=placed,
        out_specs=(P(None, AXES), P(None, AXES)),
        check_vma=False,
    )
```

```python
import functools

import jax
import jax.numpy as jnp
from jax import lax
from jax.experimental import pallas as pl
from jax.experimental.pallas import tpu as pltpu
from jax.sharding import PartitionSpec as P

LEAF_CL = 8
TOPK = 16
NEAR = 4
PARTS = 2
HALO = 4
AXES = ("group", "dev")
VMEM = pl.BlockSpec(memory_space=pltpu.VMEM)
SMEM = pl.BlockSpec(memory_space=pltpu.SMEM)
HBM = pl.BlockSpec(memory_space=pltpu.HBM)
PARAMS = pltpu.CompilerParams(vmem_limit_bytes=16 * 1024 * 1024)


def struct(shape, dtype):
    return jax.ShapeDtypeStruct(shape, dtype)


def in_hbm(*values):
    return [pltpu.with_memory_space_constraint(value, pltpu.HBM) for value in values]


def load_all(pairs, sem):
    copies = [pltpu.make_async_copy(src, dst, sem.at[at]) for at, (src, dst) in enumerate(pairs)]
    for copy in copies:
        copy.start()
    return copies


def dot_tt(left, right):
    return lax.dot_general(
        left, right, (((1,), (1,)), ((), ())), preferred_element_type=jnp.float32
    )


def dot_nn(left, right):
    return lax.dot_general(
        left, right, (((1,), (0,)), ((), ())), preferred_element_type=jnp.float32
    )


def split(value):
    high = value.astype(jnp.bfloat16)
    low = (value - high.astype(jnp.float32)).astype(jnp.bfloat16)
    return jnp.concatenate([high, low], axis=0)


def send_chunk(chunk_hbm, chunk_ref, sem, parts):
    for at in range(len(parts) // 2):
        pair = jnp.concatenate(parts[2 * at : 2 * at + 2], axis=1).astype(jnp.bfloat16)
        chunk_ref[:, at] = jnp.broadcast_to(pair[None], (chunk_ref.shape[0],) + pair.shape)
    copy = pltpu.make_async_copy(chunk_ref, chunk_hbm, sem.at[0])
    copy.start()
    return copy


def put_halo(core, field_ref, inner_ref, outer_ref):
    span = inner_ref.shape[1]
    head, tail = split(field_ref[:, :span]), split(field_ref[:, field_ref.shape[1] - span :])

    @pl.when(core == 0)
    def _():
        inner_ref[...] = tail
        outer_ref[...] = head

    @pl.when(core != 0)
    def _():
        inner_ref[...] = head
        outer_ref[...] = tail


def first_kernel(
    field_hbm, basis_hbm, transfer_hbm, list_hbm, top_hbm,
    chunk_hbm, field_ref, fold_ref, inner_ref, outer_ref, place_ref, list_ref, top_ref,
    chunk_ref, chunk_sem, basis_ref, transfer_ref, rows_ref, emat_ref, sem,
):
    clusters, rank, span = fold_ref.shape
    leaves, _, leaf = basis_ref.shape
    rhs = field_ref.shape[0]
    lanes = 2 * rank
    copies = load_all(
        [
            (transfer_hbm, transfer_ref),
            (field_hbm, field_ref),
            (basis_hbm, basis_ref),
            (list_hbm, list_ref),
            (top_hbm, top_ref),
        ],
        sem,
    )
    device = lax.axis_index("dev")
    place_ref[0] = (lax.axis_index("group") * lax.axis_size("dev") + device) * leaves
    place_ref[1] = device % 2
    copies[0].wait()
    for j in range(rank // 2):
        rows_ref[j * leaves : (j + 1) * leaves] = transfer_ref[:, j * lanes : (j + 1) * lanes].astype(jnp.float32)
    for i in range(leaves):
        rows = rows_ref[pl.ds(i, rank // 2, stride=leaves), :]
        emat_ref[i, pl.ds(0, rank // 2, stride=2), :] = rows
        emat_ref[i, pl.ds(1, rank // 2, stride=2), :] = pltpu.roll(rows, rank, 1)
    copies[1].wait()
    copies[2].wait()
    cells = split(field_ref[...])
    folds = []
    for c in range(clusters):
        tiles = []
        for i in range(c * LEAF_CL, (c + 1) * LEAF_CL):
            emat = emat_ref[i][:, :rank].astype(jnp.bfloat16)
            fold = lax.dot_general(
                emat, basis_ref[i], (((0,), (0,)), ((), ())), preferred_element_type=jnp.float32
            )
            tiles.append(fold.astype(jnp.bfloat16))
        folds.append(jnp.concatenate(tiles, axis=1))
    parts = [halves_sum(dot_tt(cells[:, c * span : (c + 1) * span], fold)) for c, fold in enumerate(folds)]
    sent = send_chunk(chunk_hbm, chunk_ref, chunk_sem, parts)
    for c, fold in enumerate(folds):
        fold_ref[c] = fold
    put_halo(device % 2, field_ref, inner_ref, outer_ref)
    copies[3].wait()
    copies[4].wait()
    sent.wait()


def prepare_kernel(
    place_ref, list_ref, field_ref, fold_ref, coupling_hbm, blocks_hbm,
    near_ref, ends_ref, smat_ref, turned_ref, gram_ref, table, blocks_ref, coupling_ref, rows_ref, sem
):
    pairs, each = part_copies(blocks_hbm, blocks_ref)
    copies = load_all([(coupling_hbm, coupling_ref)] + pairs, sem)
    clusters, rank, span = fold_ref.shape
    half = rank // 2
    row = lax.broadcasted_iota(jnp.int32, (rank, rank), 0)
    column = lax.broadcasted_iota(jnp.int32, (rank, rank), 1)
    order = (column == 2 * (row % half) + row // half).astype(jnp.bfloat16)
    for c in range(clusters):
        turned = dot_nn(order, fold_ref[c]).astype(jnp.bfloat16)
        turned_ref[c] = turned
        gram_ref[c] = dot_tt(turned, fold_ref[c]).astype(jnp.bfloat16)
    copies[0].wait()
    lower = lax.broadcasted_iota(jnp.int32, (half, 2 * rank), 1) < rank
    for c in range(clusters):
        for j in range(half):
            rows_ref[j * TOPK : (j + 1) * TOPK] = coupling_ref[c, :, j * 2 * rank : (j + 1) * 2 * rank].astype(jnp.float32)
        for k in range(0, TOPK, 2):
            one = rows_ref[pl.ds(k, half, stride=TOPK), :]
            two = rows_ref[pl.ds(k + 1, half, stride=TOPK), :]
            even = jnp.where(lower, one, pltpu.roll(two, rank, 1))
            odd = jnp.where(lower, pltpu.roll(one, rank, 1), two)
            smat_ref[c, :, k * rank : (k + 2) * rank] = jnp.concatenate([even, odd], axis=0).astype(jnp.bfloat16)
    ready = wait_parts(copies[1:], each)
    near_sum(place_ref, list_ref, field_ref, blocks_ref, near_ref, ends_ref, table, ready)


def halves_sum(total):
    rhs = total.shape[0] // 2
    return total[:rhs] + total[rhs:]


def near_sum(place_ref, list_ref, field_ref, blocks_ref, near_ref, ends_ref, table, ready):
    leaves, _, leaf, _ = blocks_ref.shape
    for i in range(leaves):
        table[i] = split(field_ref[:, i * leaf : (i + 1) * leaf])
    table[leaves] = jnp.zeros(table.shape[1:], table.dtype)
    first = place_ref[0]
    for i in range(leaves):
        ready(min(i + HALO, leaves - 1))
        values, blocks = [], []
        for k in range(NEAR):
            at = list_ref[k, i] - first
            inside = (at >= 0) & (at < leaves)
            values.append(table[jnp.where(inside, at, leaves)])
            blocks.append(blocks_ref[jnp.where(inside, at, i), k])
        total = dot_nn(jnp.concatenate(values, axis=1), jnp.concatenate(blocks, axis=0))
        near_ref[:, i * leaf : (i + 1) * leaf] = halves_sum(total)
    ends_ref[:HALO] = blocks_ref[:HALO]
    ends_ref[HALO:] = blocks_ref[leaves - HALO :]


def wait_parts(copies, each):
    done = []

    def ready(leaf):
        while len(done) <= leaf // each:
            copies[len(done)].wait()
            done.append(leaf)

    return ready


def part_copies(blocks_hbm, blocks_ref):
    each = blocks_ref.shape[0] // PARTS
    spans = [pl.ds(at * each, each) for at in range(PARTS)]
    return [(blocks_hbm.at[at], blocks_ref.at[at]) for at in spans], each


def near_kernel(
    place_ref, list_ref, field_ref, blocks_hbm, near_ref, ends_ref, table, blocks_ref, sem
):
    pairs, each = part_copies(blocks_hbm, blocks_ref)
    ready = wait_parts(load_all(pairs, sem), each)
    near_sum(place_ref, list_ref, field_ref, blocks_ref, near_ref, ends_ref, table, ready)


def edge_kernel(leaves, place_ref, list_ref, inner_ref, outer_ref, ends_ref, edge_ref, table):
    leaf = ends_ref.shape[2]
    zero = 2 * HALO
    table[zero] = jnp.zeros(table.shape[1:], table.dtype)
    even = jnp.where(place_ref[1] == 0, HALO, 0)
    for i in range(HALO):
        table[even + i] = inner_ref[:, i * leaf : (i + 1) * leaf]
        table[HALO - even + i] = outer_ref[:, i * leaf : (i + 1) * leaf]
    first = place_ref[0]
    for i in range(2 * HALO):
        own = i if i < HALO else leaves - 2 * HALO + i

        def pick(k):
            at = list_ref[k, own] - first
            return table[jnp.where(at < 0, at + HALO, jnp.where(at >= leaves, at - leaves + HALO, zero))]

        values = jnp.concatenate([pick(k) for k in range(NEAR)], axis=1)
        blocks = jnp.concatenate([ends_ref[i, k] for k in range(NEAR)], axis=1)
        edge_ref[:, i * leaf : (i + 1) * leaf] = halves_sum(dot_tt(values, blocks))


def near_part(c, clusters, near_ref, edge_ref):
    span = near_ref.shape[1] // clusters
    near = near_ref[:, c * span : (c + 1) * span]
    half = edge_ref.shape[1] // 2
    rest = jnp.zeros((near.shape[0], span - half), jnp.float32)
    if c == 0:
        near += jnp.concatenate([edge_ref[:, :half], rest], axis=1)
    if c == clusters - 1:
        near += jnp.concatenate([rest, edge_ref[:, half:]], axis=1)
    return near


def down_parts(top_ref, table_ref, smat_ref):
    shape = table_ref.shape[1:]
    rank = shape[1] // 2
    lower = lax.broadcasted_iota(jnp.int32, shape, 1) < rank

    def pick(c, k):
        top = top_ref[c, k]
        tile = table_ref[top >> 1]
        turned = jnp.concatenate([tile[:, rank:], tile[:, :rank]], axis=1)
        return jnp.where(jnp.broadcast_to(top & 1, shape) == k % 2, tile, turned)

    downs = []
    for c in range(smat_ref.shape[0]):
        tiles = [jnp.where(lower, pick(c, k), pick(c, k + 1)) for k in range(0, TOPK, 2)]
        downs.append(dot_tt(jnp.concatenate(tiles, axis=1), smat_ref[c]).astype(jnp.bfloat16))
    return downs


def second_kernel(
    place_ref, top_ref, table_ref, smat_ref, turned_ref, gram_ref, fold_ref, nugget_ref, field_ref, near_ref, edge_ref,
    chunk_hbm, image_ref, inner_ref, outer_ref, chunk_ref, sem,
):
    clusters, _, span = fold_ref.shape
    spans = [slice(c * span, (c + 1) * span) for c in range(clusters)]
    downs = down_parts(top_ref, table_ref, smat_ref)
    bases, parts = [], []
    for c, at in enumerate(spans):
        bases.append(nugget_ref[:, at] * field_ref[:, at] + near_part(c, clusters, near_ref, edge_ref))
        parts.append(halves_sum(dot_tt(split(bases[c]), fold_ref[c])))
    parts = [part + dot_nn(down, gram_ref[c]) for c, (part, down) in enumerate(zip(parts, downs))]
    sent = send_chunk(chunk_hbm, chunk_ref, sem, parts)
    for c, at in enumerate(spans):
        image_ref[:, at] = bases[c] + dot_nn(downs[c], turned_ref[c])
    put_halo(place_ref[1], image_ref, inner_ref, outer_ref)
    sent.wait()


def third_kernel(
    top_ref, table_ref, smat_ref, turned_ref, nugget_ref, field_ref, image_ref, near_ref, edge_ref,
    twice_ref, sums_ref,
):
    clusters, _, span = turned_ref.shape
    rhs = field_ref.shape[0]
    for c, down in enumerate(down_parts(top_ref, table_ref, smat_ref)):
        at = slice(c * span, (c + 1) * span)
        far = dot_nn(down, turned_ref[c])
        near = near_part(c, clusters, near_ref, edge_ref)
        twice_ref[:, at] = nugget_ref[:, at] * image_ref[:, at] + near + far

    def dot(left, right):
        return jnp.sum(left * right, axis=1, keepdims=True)

    field, image, twice = field_ref[...], image_ref[...], twice_ref[...]
    size = dot(image, image)
    cross = dot(field, image)
    own = cross / jnp.where(size > 0, size, 1.0)
    rest = field - own * image
    bent = image - own * twice
    sums = [
        dot(field, field),
        cross,
        size,
        dot(rest, rest),
        dot(rest, bent),
        dot(image, bent) + dot(rest, twice),
        dot(image, twice),
    ]
    width = sums_ref.shape[2]
    lane = lax.broadcasted_iota(jnp.int32, (rhs, width), 1)
    row = lax.broadcasted_iota(jnp.int32, (rhs, width), 0)
    packed = jnp.zeros((rhs, width), jnp.float32)
    for at, value in enumerate(sums):
        packed = jnp.where(lane == row + at * rhs, value, packed)
    flat = jnp.sum(packed, axis=0, keepdims=True)
    sums_ref[...] = jnp.broadcast_to(flat[None], sums_ref.shape)


def last_kernel(sums_ref, field_ref, image_ref, twice_ref, solution_ref, residual_ref):
    rhs = field_ref.shape[0]
    sums = sums_ref[...].reshape(sums_ref.shape[0], sums_ref.shape[2]).T

    def part(at):
        return sums[at * rhs : (at + 1) * rhs]

    def total(value):
        return jnp.sum(value, axis=1, keepdims=True)

    norm = total(part(0))
    curve = total(part(1))
    size = part(2)
    own = part(1) / jnp.where(size > 0, size, 1.0)
    alpha = norm / curve
    delta = own - alpha
    norm_next = total(part(3) + delta * delta * size)
    rest_bent = total(part(4) + delta * (part(5) + delta * part(6)))
    rest_image = total(delta * size)
    beta = norm_next / norm
    curve_next = rest_bent + beta * (2.0 * rest_image + beta * curve)
    alpha_next = norm_next / curve_next
    outer = alpha + alpha_next * (1.0 + beta)
    inner = alpha * alpha_next
    field, image = field_ref[...], image_ref[...]
    solution_ref[...] = outer * field - inner * image
    residual_ref[...] = field - outer * image + inner * twice_ref[...]


def exchange(chunk):
    return lax.all_to_all(chunk, AXES, 0, 0)


def swap_cores(value):
    return lax.ppermute(value, "dev", [(i, i ^ 1) for i in range(lax.axis_size("dev"))])


def swap_ends(inner, outer):
    count = lax.axis_size("dev")
    inner = swap_cores(inner)
    pairs = [(i, i + 1) for i in range(1, count - 1, 2)]
    outer = lax.ppermute(outer, "dev", pairs + [(b, a) for a, b in pairs])
    return inner, outer


def per_device(right_side, nugget, near_blocks, near_list, basis, transfer, coupling, top_list):
    rhs, width = right_side.shape
    leaves, rank, leaf = basis.shape
    clusters = coupling.shape[0]
    span = leaf * LEAF_CL
    devices = lax.axis_size("group") * lax.axis_size("dev")
    nugget = nugget[None]
    chunk_shape = pltpu.HBM((devices, clusters // 2, rhs, 2 * rank), jnp.bfloat16)
    chunk_scratch = [pltpu.VMEM(chunk_shape.shape, jnp.bfloat16), pltpu.SemaphoreType.DMA((1,))]
    end = HALO * leaf
    field_shape = pltpu.VMEM((rhs, width), jnp.float32)
    fold_shape = pltpu.VMEM((clusters, rank, span), jnp.bfloat16)
    end_shape = pltpu.VMEM((2 * rhs, end), jnp.bfloat16)

    chunk, field, fold, inner, outer, place, near_list, top_list = pl.pallas_call(
        first_kernel,
        in_specs=[HBM] * 5,
        out_specs=[HBM] + [VMEM] * 4 + [SMEM] * 3,
        out_shape=[
            chunk_shape,
            field_shape,
            fold_shape,
            end_shape,
            end_shape,
            pltpu.SMEM((2,), jnp.int32),
            pltpu.SMEM(near_list.T.shape, near_list.dtype),
            pltpu.SMEM(top_list.shape, top_list.dtype),
        ],
        scratch_shapes=chunk_scratch
        + [
            pltpu.VMEM(basis.shape, basis.dtype),
            pltpu.VMEM(transfer.shape, transfer.dtype),
            pltpu.VMEM((leaves * rank // 2, 2 * rank), jnp.float32),
            pltpu.VMEM((leaves, rank, 2 * rank), jnp.float32),
            pltpu.SemaphoreType.DMA((5,)),
        ],
        compiler_params=PARAMS,
        name="first",
    )(*in_hbm(right_side, basis, transfer, near_list.T, top_list))
    table = exchange(chunk).reshape(-1, rhs, 2 * rank)
    ends_shape = pltpu.VMEM((2 * HALO,) + near_blocks.shape[1:], near_blocks.dtype)
    near_scratch = [
        pltpu.VMEM((leaves + 1, 2 * rhs, leaf), jnp.bfloat16),
        pltpu.VMEM(near_blocks.shape, near_blocks.dtype),
    ]

    def edge_product(inner, outer, ends):
        return pl.pallas_call(
            functools.partial(edge_kernel, leaves),
            in_specs=[SMEM] * 2 + [VMEM] * 3,
            out_specs=VMEM,
            out_shape=pltpu.VMEM((rhs, 2 * end), jnp.float32),
            scratch_shapes=[pltpu.VMEM((2 * HALO + 1, 2 * rhs, leaf), jnp.bfloat16)],
            compiler_params=PARAMS,
            name="edge",
        )(place, near_list, *swap_ends(inner, outer), ends)

    near, ends, smat, turned, gram = pl.pallas_call(
        prepare_kernel,
        in_specs=[SMEM] * 2 + [VMEM] * 2 + [HBM] * 2,
        out_specs=[VMEM] * 5,
        out_shape=[
            field_shape,
            ends_shape,
            pltpu.VMEM((clusters, rank, TOPK * rank), jnp.bfloat16),
            fold_shape,
            pltpu.VMEM((clusters, rank, rank), jnp.bfloat16),
        ],
        scratch_shapes=near_scratch
        + [
            pltpu.VMEM(coupling.shape, coupling.dtype),
            pltpu.VMEM((rank // 2 * TOPK, 2 * rank), jnp.float32),
            pltpu.SemaphoreType.DMA((1 + PARTS,)),
        ],
        compiler_params=PARAMS,
        name="prepare",
    )(place, near_list, field, fold, *in_hbm(coupling, near_blocks))
    edge = edge_product(inner, outer, ends)

    chunk, image, inner, outer = pl.pallas_call(
        second_kernel,
        in_specs=[SMEM] * 2 + [VMEM] * 9,
        out_specs=[HBM] + [VMEM] * 3,
        out_shape=[chunk_shape, field_shape, end_shape, end_shape],
        scratch_shapes=chunk_scratch,
        compiler_params=PARAMS,
        name="second",
    )(place, top_list, table, smat, turned, gram, fold, nugget, field, near, edge)
    table = exchange(chunk).reshape(-1, rhs, 2 * rank)
    near, ends = pl.pallas_call(
        near_kernel,
        in_specs=[SMEM] * 2 + [VMEM, HBM],
        out_specs=[VMEM] * 2,
        out_shape=[field_shape, ends_shape],
        scratch_shapes=near_scratch + [pltpu.SemaphoreType.DMA((PARTS,))],
        compiler_params=PARAMS,
        name="near",
    )(place, near_list, image, *in_hbm(near_blocks))
    edge = edge_product(inner, outer, ends)

    twice, sums = pl.pallas_call(
        third_kernel,
        in_specs=[SMEM] + [VMEM] * 8,
        out_specs=[VMEM] * 2,
        out_shape=[field_shape, struct((devices, 1, 8 * rhs), jnp.float32)],
        compiler_params=PARAMS,
        name="third",
    )(top_list, table, smat, turned, nugget, field, image, near, edge)
    sums = exchange(sums)

    return pl.pallas_call(
        last_kernel,
        in_specs=[VMEM] * 4,
        out_specs=[VMEM] * 2,
        out_shape=[struct((rhs, width), jnp.float32)] * 2,
        compiler_params=PARAMS,
        name="last",
    )(sums, field, image, twice)


def solution(mesh):
    placed = (
        P(None, AXES),
        P(AXES),
        P(AXES, None, None, None),
        P(AXES, None),
        P(AXES, None, None),
        P(AXES, None),
        P(AXES, None, None),
        P(AXES, None),
    )
    return jax.shard_map(
        per_device,
        mesh=mesh,
        in_specs=placed,
        out_specs=(P(None, AXES), P(None, AXES)),
        check_vma=False,
    )
```

```python
import functools

import jax
import jax.numpy as jnp
from jax import lax
from jax.experimental import pallas as pl
from jax.experimental.pallas import tpu as pltpu
from jax.sharding import PartitionSpec as P

LEAF_CL = 8
TOPK = 16
NEAR = 4
PARTS = 2
HALO = 4
AXES = ("group", "dev")
VMEM = pl.BlockSpec(memory_space=pltpu.VMEM)
SMEM = pl.BlockSpec(memory_space=pltpu.SMEM)
HBM = pl.BlockSpec(memory_space=pltpu.HBM)
PARAMS = pltpu.CompilerParams(vmem_limit_bytes=16 * 1024 * 1024)


def struct(shape, dtype):
    return jax.ShapeDtypeStruct(shape, dtype)


def in_hbm(*values):
    return [pltpu.with_memory_space_constraint(value, pltpu.HBM) for value in values]


def load_all(pairs, sem):
    copies = [pltpu.make_async_copy(src, dst, sem.at[at]) for at, (src, dst) in enumerate(pairs)]
    for copy in copies:
        copy.start()
    return copies


def dot_tt(left, right):
    return lax.dot_general(
        left, right, (((1,), (1,)), ((), ())), preferred_element_type=jnp.float32
    )


def dot_nn(left, right):
    return lax.dot_general(
        left, right, (((1,), (0,)), ((), ())), preferred_element_type=jnp.float32
    )


def split(value):
    high = value.astype(jnp.bfloat16)
    low = (value - high.astype(jnp.float32)).astype(jnp.bfloat16)
    return jnp.concatenate([high, low], axis=0)


def send_chunk(chunk_hbm, chunk_ref, sem, parts):
    for at in range(len(parts) // 2):
        pair = jnp.concatenate(parts[2 * at : 2 * at + 2], axis=1).astype(jnp.bfloat16)
        chunk_ref[:, at] = jnp.broadcast_to(pair[None], (chunk_ref.shape[0],) + pair.shape)
    copy = pltpu.make_async_copy(chunk_ref, chunk_hbm, sem.at[0])
    copy.start()
    return copy


def put_halo(core, field_ref, inner_ref, outer_ref):
    span = inner_ref.shape[1]
    head, tail = split(field_ref[:, :span]), split(field_ref[:, field_ref.shape[1] - span :])

    @pl.when(core == 0)
    def _():
        inner_ref[...] = tail
        outer_ref[...] = head

    @pl.when(core != 0)
    def _():
        inner_ref[...] = head
        outer_ref[...] = tail


def first_kernel(
    field_hbm, basis_hbm, transfer_hbm, list_hbm, top_hbm,
    chunk_hbm, field_ref, fold_ref, inner_ref, outer_ref, place_ref, list_ref, top_ref,
    chunk_ref, chunk_sem, basis_ref, transfer_ref, rows_ref, emat_ref, sem,
):
    clusters, rank, span = fold_ref.shape
    leaves, _, leaf = basis_ref.shape
    rhs = field_ref.shape[0]
    lanes = 2 * rank
    copies = load_all(
        [
            (transfer_hbm, transfer_ref),
            (field_hbm, field_ref),
            (basis_hbm, basis_ref),
            (list_hbm, list_ref),
            (top_hbm, top_ref),
        ],
        sem,
    )
    device = lax.axis_index("dev")
    place_ref[0] = (lax.axis_index("group") * lax.axis_size("dev") + device) * leaves
    place_ref[1] = device % 2
    copies[0].wait()
    for j in range(rank // 2):
        rows_ref[j * leaves : (j + 1) * leaves] = transfer_ref[:, j * lanes : (j + 1) * lanes].astype(jnp.float32)
    for i in range(leaves):
        rows = rows_ref[pl.ds(i, rank // 2, stride=leaves), :]
        emat_ref[i, pl.ds(0, rank // 2, stride=2), :] = rows
        emat_ref[i, pl.ds(1, rank // 2, stride=2), :] = pltpu.roll(rows, rank, 1)
    copies[1].wait()
    copies[2].wait()
    cells = split(field_ref[...])
    folds = []
    for c in range(clusters):
        tiles = []
        for i in range(c * LEAF_CL, (c + 1) * LEAF_CL):
            emat = emat_ref[i][:, :rank].astype(jnp.bfloat16)
            fold = lax.dot_general(
                emat, basis_ref[i], (((0,), (0,)), ((), ())), preferred_element_type=jnp.float32
            )
            tiles.append(fold.astype(jnp.bfloat16))
        folds.append(jnp.concatenate(tiles, axis=1))
    parts = [halves_sum(dot_tt(cells[:, c * span : (c + 1) * span], fold)) for c, fold in enumerate(folds)]
    sent = send_chunk(chunk_hbm, chunk_ref, chunk_sem, parts)
    for c, fold in enumerate(folds):
        fold_ref[c] = fold
    put_halo(device % 2, field_ref, inner_ref, outer_ref)
    copies[3].wait()
    copies[4].wait()
    sent.wait()


def prepare_kernel(
    place_ref, list_ref, field_ref, fold_ref, coupling_hbm, blocks_hbm,
    near_ref, ends_ref, smat_ref, turned_ref, gram_ref, table, blocks_ref, coupling_ref, rows_ref, sem
):
    pairs, each = part_copies(blocks_hbm, blocks_ref)
    copies = load_all([(coupling_hbm, coupling_ref)] + pairs, sem)
    clusters, rank, span = fold_ref.shape
    half = rank // 2
    row = lax.broadcasted_iota(jnp.int32, (rank, rank), 0)
    column = lax.broadcasted_iota(jnp.int32, (rank, rank), 1)
    order = (column == 2 * (row % half) + row // half).astype(jnp.bfloat16)
    for c in range(clusters):
        turned = dot_nn(order, fold_ref[c]).astype(jnp.bfloat16)
        turned_ref[c] = turned
        gram_ref[c] = dot_tt(turned, fold_ref[c]).astype(jnp.bfloat16)
    copies[0].wait()
    lower = lax.broadcasted_iota(jnp.int32, (half, 2 * rank), 1) < rank
    for c in range(clusters):
        for j in range(half):
            rows_ref[j * TOPK : (j + 1) * TOPK] = coupling_ref[c, :, j * 2 * rank : (j + 1) * 2 * rank].astype(jnp.float32)
        for k in range(0, TOPK, 2):
            one = rows_ref[pl.ds(k, half, stride=TOPK), :]
            two = rows_ref[pl.ds(k + 1, half, stride=TOPK), :]
            even = jnp.where(lower, one, pltpu.roll(two, rank, 1))
            odd = jnp.where(lower, pltpu.roll(one, rank, 1), two)
            smat_ref[c, :, k * rank : (k + 2) * rank] = jnp.concatenate([even, odd], axis=0).astype(jnp.bfloat16)
    ready = wait_parts(copies[1:], each)
    near_sum(place_ref, list_ref, field_ref, blocks_ref, near_ref, ends_ref, table, ready)


def halves_sum(total):
    rhs = total.shape[0] // 2
    return total[:rhs] + total[rhs:]


def near_sum(place_ref, list_ref, field_ref, blocks_ref, near_ref, ends_ref, table, ready):
    leaves, _, leaf, _ = blocks_ref.shape
    for i in range(leaves):
        table[i] = split(field_ref[:, i * leaf : (i + 1) * leaf])
    table[leaves] = jnp.zeros(table.shape[1:], table.dtype)
    first = place_ref[0]
    for i in range(leaves):
        ready(min(i + HALO, leaves - 1))
        values, blocks = [], []
        for k in range(NEAR):
            at = list_ref[k, i] - first
            inside = (at >= 0) & (at < leaves)
            values.append(table[jnp.where(inside, at, leaves)])
            blocks.append(blocks_ref[jnp.where(inside, at, i), k])
        total = dot_nn(jnp.concatenate(values, axis=1), jnp.concatenate(blocks, axis=0))
        near_ref[:, i * leaf : (i + 1) * leaf] = halves_sum(total)
    ends_ref[:HALO] = blocks_ref[:HALO]
    ends_ref[HALO:] = blocks_ref[leaves - HALO :]


def wait_parts(copies, each):
    done = []

    def ready(leaf):
        while len(done) <= leaf // each:
            copies[len(done)].wait()
            done.append(leaf)

    return ready


def part_copies(blocks_hbm, blocks_ref):
    each = blocks_ref.shape[0] // PARTS
    spans = [pl.ds(at * each, each) for at in range(PARTS)]
    return [(blocks_hbm.at[at], blocks_ref.at[at]) for at in spans], each


def near_kernel(
    place_ref, list_ref, field_ref, start_ref, blocks_hbm, near_ref, ends_ref, rest_ref, table, blocks_ref, sem
):
    pairs, each = part_copies(blocks_hbm, blocks_ref)
    ready = wait_parts(load_all(pairs, sem), each)
    near_sum(place_ref, list_ref, field_ref, blocks_ref, near_ref, ends_ref, table, ready)
    start, field = start_ref[...], field_ref[...]
    size = jnp.sum(field * field, axis=1, keepdims=True)
    cross = jnp.sum(start * field, axis=1, keepdims=True)
    rest_ref[...] = start - cross / jnp.where(size > 0, size, 1.0) * field


def edge_kernel(leaves, place_ref, list_ref, inner_ref, outer_ref, ends_ref, edge_ref, table):
    leaf = ends_ref.shape[2]
    zero = 2 * HALO
    table[zero] = jnp.zeros(table.shape[1:], table.dtype)
    even = jnp.where(place_ref[1] == 0, HALO, 0)
    for i in range(HALO):
        table[even + i] = inner_ref[:, i * leaf : (i + 1) * leaf]
        table[HALO - even + i] = outer_ref[:, i * leaf : (i + 1) * leaf]
    first = place_ref[0]
    for i in range(2 * HALO):
        own = i if i < HALO else leaves - 2 * HALO + i

        def pick(k):
            at = list_ref[k, own] - first
            return table[jnp.where(at < 0, at + HALO, jnp.where(at >= leaves, at - leaves + HALO, zero))]

        values = jnp.concatenate([pick(k) for k in range(NEAR)], axis=1)
        blocks = jnp.concatenate([ends_ref[i, k] for k in range(NEAR)], axis=1)
        edge_ref[:, i * leaf : (i + 1) * leaf] = halves_sum(dot_tt(values, blocks))


def near_part(c, clusters, near_ref, edge_ref):
    span = near_ref.shape[1] // clusters
    near = near_ref[:, c * span : (c + 1) * span]
    half = edge_ref.shape[1] // 2
    rest = jnp.zeros((near.shape[0], span - half), jnp.float32)
    if c == 0:
        near += jnp.concatenate([edge_ref[:, :half], rest], axis=1)
    if c == clusters - 1:
        near += jnp.concatenate([rest, edge_ref[:, half:]], axis=1)
    return near


def down_parts(top_ref, table_ref, smat_ref):
    shape = table_ref.shape[1:]
    rank = shape[1] // 2
    lower = lax.broadcasted_iota(jnp.int32, shape, 1) < rank

    def pick(c, k):
        top = top_ref[c, k]
        tile = table_ref[top >> 1]
        turned = jnp.concatenate([tile[:, rank:], tile[:, :rank]], axis=1)
        return jnp.where(jnp.broadcast_to(top & 1, shape) == k % 2, tile, turned)

    downs = []
    for c in range(smat_ref.shape[0]):
        tiles = [jnp.where(lower, pick(c, k), pick(c, k + 1)) for k in range(0, TOPK, 2)]
        downs.append(dot_tt(jnp.concatenate(tiles, axis=1), smat_ref[c]).astype(jnp.bfloat16))
    return downs


def second_kernel(
    place_ref, top_ref, table_ref, smat_ref, turned_ref, gram_ref, fold_ref, nugget_ref, field_ref, near_ref, edge_ref,
    chunk_hbm, image_ref, inner_ref, outer_ref, chunk_ref, sem,
):
    clusters, _, span = fold_ref.shape
    spans = [slice(c * span, (c + 1) * span) for c in range(clusters)]
    downs = down_parts(top_ref, table_ref, smat_ref)
    bases, parts = [], []
    for c, at in enumerate(spans):
        bases.append(nugget_ref[:, at] * field_ref[:, at] + near_part(c, clusters, near_ref, edge_ref))
        parts.append(halves_sum(dot_tt(split(bases[c]), fold_ref[c])))
    parts = [part + dot_nn(down, gram_ref[c]) for c, (part, down) in enumerate(zip(parts, downs))]
    sent = send_chunk(chunk_hbm, chunk_ref, sem, parts)
    for c, at in enumerate(spans):
        image_ref[:, at] = bases[c] + dot_nn(downs[c], turned_ref[c])
    put_halo(place_ref[1], image_ref, inner_ref, outer_ref)
    sent.wait()


def third_kernel(
    top_ref, table_ref, smat_ref, turned_ref, nugget_ref, field_ref, image_ref, rest_ref, near_ref, edge_ref,
    twice_ref, sums_ref,
):
    clusters, _, span = turned_ref.shape
    rhs = field_ref.shape[0]
    for c, down in enumerate(down_parts(top_ref, table_ref, smat_ref)):
        at = slice(c * span, (c + 1) * span)
        far = dot_nn(down, turned_ref[c])
        near = near_part(c, clusters, near_ref, edge_ref)
        twice_ref[:, at] = nugget_ref[:, at] * image_ref[:, at] + near + far

    def dot(left, right):
        return jnp.sum(left * right, axis=1, keepdims=True)

    field, image, twice = field_ref[...], image_ref[...], twice_ref[...]
    rest = rest_ref[...]
    size = dot(image, image)
    cross = dot(field, image)
    rest_twice, image_twice = dot(rest, twice), dot(image, twice)
    own = cross / jnp.where(size > 0, size, 1.0)
    sums = [
        dot(field, field),
        cross,
        size,
        dot(rest, rest),
        dot(rest, image) - own * rest_twice,
        size - own * image_twice + rest_twice,
        image_twice,
    ]
    width = sums_ref.shape[2]
    lane = lax.broadcasted_iota(jnp.int32, (rhs, width), 1)
    row = lax.broadcasted_iota(jnp.int32, (rhs, width), 0)
    packed = jnp.zeros((rhs, width), jnp.float32)
    for at, value in enumerate(sums):
        packed = jnp.where(lane == row + at * rhs, value, packed)
    flat = jnp.sum(packed, axis=0, keepdims=True)
    sums_ref[...] = jnp.broadcast_to(flat[None], sums_ref.shape)


def last_kernel(sums_ref, field_ref, image_ref, twice_ref, solution_ref, residual_ref):
    rhs = field_ref.shape[0]
    sums = sums_ref[...].reshape(sums_ref.shape[0], sums_ref.shape[2]).T

    def part(at):
        return sums[at * rhs : (at + 1) * rhs]

    def total(value):
        return jnp.sum(value, axis=1, keepdims=True)

    norm = total(part(0))
    curve = total(part(1))
    size = part(2)
    own = part(1) / jnp.where(size > 0, size, 1.0)
    alpha = norm / curve
    delta = own - alpha
    norm_next = total(part(3) + delta * delta * size)
    rest_bent = total(part(4) + delta * (part(5) + delta * part(6)))
    rest_image = total(delta * size)
    beta = norm_next / norm
    curve_next = rest_bent + beta * (2.0 * rest_image + beta * curve)
    alpha_next = norm_next / curve_next
    outer = alpha + alpha_next * (1.0 + beta)
    inner = alpha * alpha_next
    field, image = field_ref[...], image_ref[...]
    solution_ref[...] = outer * field - inner * image
    residual_ref[...] = field - outer * image + inner * twice_ref[...]


def exchange(chunk):
    return lax.all_to_all(chunk, AXES, 0, 0)


def swap_cores(value):
    return lax.ppermute(value, "dev", [(i, i ^ 1) for i in range(lax.axis_size("dev"))])


def swap_ends(inner, outer):
    count = lax.axis_size("dev")
    inner = swap_cores(inner)
    pairs = [(i, i + 1) for i in range(1, count - 1, 2)]
    outer = lax.ppermute(outer, "dev", pairs + [(b, a) for a, b in pairs])
    return inner, outer


def per_device(right_side, nugget, near_blocks, near_list, basis, transfer, coupling, top_list):
    rhs, width = right_side.shape
    leaves, rank, leaf = basis.shape
    clusters = coupling.shape[0]
    span = leaf * LEAF_CL
    devices = lax.axis_size("group") * lax.axis_size("dev")
    nugget = nugget[None]
    chunk_shape = pltpu.HBM((devices, clusters // 2, rhs, 2 * rank), jnp.bfloat16)
    chunk_scratch = [pltpu.VMEM(chunk_shape.shape, jnp.bfloat16), pltpu.SemaphoreType.DMA((1,))]
    end = HALO * leaf
    field_shape = pltpu.VMEM((rhs, width), jnp.float32)
    fold_shape = pltpu.VMEM((clusters, rank, span), jnp.bfloat16)
    end_shape = pltpu.VMEM((2 * rhs, end), jnp.bfloat16)

    chunk, field, fold, inner, outer, place, near_list, top_list = pl.pallas_call(
        first_kernel,
        in_specs=[HBM] * 5,
        out_specs=[HBM] + [VMEM] * 4 + [SMEM] * 3,
        out_shape=[
            chunk_shape,
            field_shape,
            fold_shape,
            end_shape,
            end_shape,
            pltpu.SMEM((2,), jnp.int32),
            pltpu.SMEM(near_list.T.shape, near_list.dtype),
            pltpu.SMEM(top_list.shape, top_list.dtype),
        ],
        scratch_shapes=chunk_scratch
        + [
            pltpu.VMEM(basis.shape, basis.dtype),
            pltpu.VMEM(transfer.shape, transfer.dtype),
            pltpu.VMEM((leaves * rank // 2, 2 * rank), jnp.float32),
            pltpu.VMEM((leaves, rank, 2 * rank), jnp.float32),
            pltpu.SemaphoreType.DMA((5,)),
        ],
        compiler_params=PARAMS,
        name="first",
    )(*in_hbm(right_side, basis, transfer, near_list.T, top_list))
    table = exchange(chunk).reshape(-1, rhs, 2 * rank)
    ends_shape = pltpu.VMEM((2 * HALO,) + near_blocks.shape[1:], near_blocks.dtype)
    near_scratch = [
        pltpu.VMEM((leaves + 1, 2 * rhs, leaf), jnp.bfloat16),
        pltpu.VMEM(near_blocks.shape, near_blocks.dtype),
    ]

    def edge_product(inner, outer, ends):
        return pl.pallas_call(
            functools.partial(edge_kernel, leaves),
            in_specs=[SMEM] * 2 + [VMEM] * 3,
            out_specs=VMEM,
            out_shape=pltpu.VMEM((rhs, 2 * end), jnp.float32),
            scratch_shapes=[pltpu.VMEM((2 * HALO + 1, 2 * rhs, leaf), jnp.bfloat16)],
            compiler_params=PARAMS,
            name="edge",
        )(place, near_list, *swap_ends(inner, outer), ends)

    near, ends, smat, turned, gram = pl.pallas_call(
        prepare_kernel,
        in_specs=[SMEM] * 2 + [VMEM] * 2 + [HBM] * 2,
        out_specs=[VMEM] * 5,
        out_shape=[
            field_shape,
            ends_shape,
            pltpu.VMEM((clusters, rank, TOPK * rank), jnp.bfloat16),
            fold_shape,
            pltpu.VMEM((clusters, rank, rank), jnp.bfloat16),
        ],
        scratch_shapes=near_scratch
        + [
            pltpu.VMEM(coupling.shape, coupling.dtype),
            pltpu.VMEM((rank // 2 * TOPK, 2 * rank), jnp.float32),
            pltpu.SemaphoreType.DMA((1 + PARTS,)),
        ],
        compiler_params=PARAMS,
        name="prepare",
    )(place, near_list, field, fold, *in_hbm(coupling, near_blocks))
    edge = edge_product(inner, outer, ends)

    chunk, image, inner, outer = pl.pallas_call(
        second_kernel,
        in_specs=[SMEM] * 2 + [VMEM] * 9,
        out_specs=[HBM] + [VMEM] * 3,
        out_shape=[chunk_shape, field_shape, end_shape, end_shape],
        scratch_shapes=chunk_scratch,
        compiler_params=PARAMS,
        name="second",
    )(place, top_list, table, smat, turned, gram, fold, nugget, field, near, edge)
    table = exchange(chunk).reshape(-1, rhs, 2 * rank)
    near, ends, rest = pl.pallas_call(
        near_kernel,
        in_specs=[SMEM] * 2 + [VMEM] * 2 + [HBM],
        out_specs=[VMEM] * 3,
        out_shape=[field_shape, ends_shape, field_shape],
        scratch_shapes=near_scratch + [pltpu.SemaphoreType.DMA((PARTS,))],
        compiler_params=PARAMS,
        name="near",
    )(place, near_list, image, field, *in_hbm(near_blocks))
    edge = edge_product(inner, outer, ends)

    twice, sums = pl.pallas_call(
        third_kernel,
        in_specs=[SMEM] + [VMEM] * 9,
        out_specs=[VMEM] * 2,
        out_shape=[field_shape, struct((devices, 1, 8 * rhs), jnp.float32)],
        compiler_params=PARAMS,
        name="third",
    )(top_list, table, smat, turned, nugget, field, image, rest, near, edge)
    sums = exchange(sums)

    return pl.pallas_call(
        last_kernel,
        in_specs=[VMEM] * 4,
        out_specs=[VMEM] * 2,
        out_shape=[struct((rhs, width), jnp.float32)] * 2,
        compiler_params=PARAMS,
        name="last",
    )(sums, field, image, twice)


def solution(mesh):
    placed = (
        P(None, AXES),
        P(AXES),
        P(AXES, None, None, None),
        P(AXES, None),
        P(AXES, None, None),
        P(AXES, None),
        P(AXES, None, None),
        P(AXES, None),
    )
    return jax.shard_map(
        per_device,
        mesh=mesh,
        in_specs=placed,
        out_specs=(P(None, AXES), P(None, AXES)),
        check_vma=False,
    )
```
